256 devices in a mesh: sn: 64 (over z, y, core), rhs: 4 (over x).
Axes of the slice: x: 4, y: 4, z: 8, core: 2. Of those that a mesh axis runs over, the one named last changes fastest.
Arguments:
- right_sides: float32 [4, 4096, 128], P(None, 'sn', 'rhs'), may hold values from -6 to 6
- factor_below: bfloat16 [3, 4096, 4096], P(None, 'sn', 'rhs'), may hold values from -0.09375 to 0.09375
- row_blocks: int32 [3, 32, 32], replicated, may hold values from 0 to 95, as said below
- inverse_top: bfloat16 [4096, 4096], P('sn'), as said below
- inverse_second: bfloat16 [4096, 2048], P('sn'), as said below
- inverse_third: bfloat16 [4096, 1024], P('sn'), as said below
- inverse_fourth: bfloat16 [4096, 512], P('sn'), as said below
Outputs:
- solution: float32 [4, 4096, 128], P(None, 'sn', 'rhs')
The draws below stay inside these ranges and needn't reach their ends.
Inputs may be any that keep to these rules, and one draw needn't show every extreme that they name: `row_blocks`: each level-l block lists 32 distinct global blocks of the ancestors of its supernode in the binary tree (supernode s of level l has parent s // 2 of level l - 1), in any order, always including all blocks of its parent; all blocks of one supernode list the same; at level 1 they are the 32 root blocks. `inverse_top`: each supernode's block is zero below its diagonal. `inverse_second`: each supernode's block is zero below its diagonal. `inverse_third`: each supernode's block is zero below its diagonal. `inverse_fourth`: each supernode's block is zero below its diagonal.
All inputs are finite; a program needn't handle non-finite values.
Results may differ from the reference program's by a relative error of at most 0.02.
Values may be sent and summed in bfloat16 or wider, within the bound.
No kernel may reach another device: no remote copies, remote signals or barrier semaphores. Data moves between devices by JAX's collectives and lax.ppermute only.
A program may use at most 64 MiB of HBM per device.

```python
import jax
import jax.numpy as jnp
import numpy as np

BS = 128
NB = 32
LEVELS = 4
RB = 32
NRHS = 128
LEVEL_ROWS = 4096


def ancestor_table(tier_index, super_index):
    listed = []
    for upper in range(tier_index):
        ancestor = super_index >> tier_index - upper
        per_super = NB >> upper
        for offset in range(per_super):
            listed.append(upper * NB + ancestor * per_super + offset)
    return np.array(listed, dtype=np.int32)


def draw_row_blocks(key, part):
    tiers = []
    for tier_index in range(1, LEVELS):
        pieces = []
        parent_count = NB >> tier_index - 1
        for super_index in range(2 ** tier_index):
            table = ancestor_table(tier_index, super_index)
            sub_key = jax.random.fold_in(key, tier_index * 1000 + super_index)
            key_pick, key_order = jax.random.split(sub_key)
            parent_part = jnp.asarray(table[table.shape[0] - parent_count:]).astype(jnp.int32)
            extra = RB - parent_count
            if extra > 0:
                others = jnp.asarray(table[:table.shape[0] - parent_count]).astype(jnp.int32)
                order = jax.random.permutation(key_pick, others.shape[0])[:extra]
                chosen = jnp.concatenate((parent_part, others[order]), axis=0)
            else:
                chosen = parent_part
            chosen = chosen[jax.random.permutation(key_order, RB)].astype(jnp.int32)
            pieces.append(jnp.broadcast_to(chosen[None, :], (NB >> tier_index, RB)))
        tiers.append(jnp.concatenate(pieces, axis=0))
    return jnp.stack(tiers).astype(jnp.int32)


def make_inverse(key, super_width):
    level_rows = NB * BS
    row_local = lax_iota_rows(level_rows, super_width) % super_width
    col_index = jax.lax.broadcasted_iota(jnp.int32, (level_rows, super_width), 1)
    key_off, key_diag = jax.random.split(key)
    entries = jnp.clip(jax.random.normal(key_off, (level_rows, super_width), jnp.float32), -6.0, 6.0)
    entries = entries / jnp.sqrt(jnp.float32(super_width))
    diag = jnp.exp(jax.random.uniform(key_diag, (level_rows, super_width), jnp.float32, -0.69, 0.69))
    upper = jnp.where(col_index > row_local, entries, 0.0)
    result = jnp.where(col_index == row_local, diag, upper)
    return result.astype(jnp.bfloat16)


def lax_iota_rows(level_rows, super_width):
    return jax.lax.broadcasted_iota(jnp.int32, (level_rows, super_width), 0)


def draw_inverse_top(key, part):
    return make_inverse(jax.random.fold_in(key, 11), NB * BS)


def draw_inverse_second(key, part):
    return make_inverse(jax.random.fold_in(key, 12), NB * BS // 2)


def draw_inverse_third(key, part):
    return make_inverse(jax.random.fold_in(key, 13), NB * BS // 4)


def draw_inverse_fourth(key, part):
    return make_inverse(jax.random.fold_in(key, 14), NB * BS // 8)


def level_of(key, extent, shards, least, high):
    gain = 1.0
    for axis_at, blocks in shards:
        draws = jax.random.uniform(jax.random.fold_in(jax.random.fold_in(key, 6), axis_at), (blocks,), jnp.float32, least / len(shards), high / len(shards))
        gain = gain * jnp.repeat(jnp.exp(draws), extent[axis_at] // blocks).reshape((-1,) + (1,) * (len(extent) - 1 - axis_at))
    return gain


def centred(own_key, shape, deviation, bound, shards=(), held_as=jnp.bfloat16):
    gain = level_of(own_key, shape, shards, -0.22, 0.18) if shards else 1.0
    values = jax.random.normal(own_key, shape, jnp.float32) * deviation * gain
    return jnp.minimum(jnp.maximum(values, -bound), bound).astype(held_as)


def setup_inputs(seed: int = 0) -> dict:
    keys = jax.random.split(jax.random.key(seed), 8)
    return {
        "right_sides": centred(keys[0], (LEVELS, LEVEL_ROWS, NRHS), 1.0, 6.0, ((1, 64), (2, 4)), jnp.float32),
        "factor_below": centred(keys[1], (LEVELS - 1, LEVEL_ROWS, RB * BS), (RB * BS) ** -0.5, 0.09375, ((1, 64), (2, 4))),
        "row_blocks": draw_row_blocks(jax.random.fold_in(keys[7], 71), 0),
        "inverse_top": draw_inverse_top(jax.random.fold_in(keys[7], 71), 0),
        "inverse_second": draw_inverse_second(jax.random.fold_in(keys[7], 71), 0),
        "inverse_third": draw_inverse_third(jax.random.fold_in(keys[7], 71), 0),
        "inverse_fourth": draw_inverse_fourth(jax.random.fold_in(keys[7], 71), 0),
    }


def reference(right_sides, factor_below, row_blocks, inverse_top, inverse_second, inverse_third, inverse_fourth):
    inverses = (inverse_top, inverse_second, inverse_third, inverse_fourth)
    level_rows = NB * BS
    total_cols = right_sides.shape[2]
    solved = []
    outputs = []
    for tier_index in range(LEVELS):
        if tier_index == 0:
            update = right_sides[0]
        else:
            known = jnp.concatenate(solved, axis=0).reshape(tier_index * NB, BS, total_cols)
            picked = jnp.take(known, row_blocks[tier_index - 1], axis=0)
            picked = picked.reshape(NB, RB * BS, total_cols).astype(jnp.float32)
            below = factor_below[tier_index - 1].reshape(NB, BS, RB * BS).astype(jnp.float32)
            update = right_sides[tier_index] - jnp.einsum("bik,bkc->bic", below, picked).reshape(level_rows, total_cols)
        rounded = update.astype(jnp.bfloat16)
        super_width = level_rows // (2 ** tier_index)
        super_count = level_rows // super_width
        blocks_in = rounded.reshape(super_count, super_width, total_cols).astype(jnp.float32)
        inverse = inverses[tier_index].reshape(super_count, super_width, super_width).astype(jnp.float32)
        result = jnp.einsum("siw,swc->sic", inverse, blocks_in).reshape(level_rows, total_cols)
        outputs.append(result)
        solved.append(result.astype(jnp.bfloat16))
    return jnp.stack(outputs)
```

```python
import functools

import jax
import jax.numpy as jnp
from jax import lax
from jax.experimental import pallas as pl
from jax.experimental.pallas import tpu as pltpu
from jax.sharding import PartitionSpec as P

BS = 128
NB = 32
LEVELS = 4
RB = 32


def pack(block, copies):
    flipped = block.T
    half = flipped.shape[0] // 2
    packed = jnp.concatenate((flipped[:half], flipped[half:]), axis=1).astype(jnp.bfloat16)
    return jnp.broadcast_to(packed[None], (copies, *packed.shape))


def unpack(gathered, store):
    lanes = gathered.shape[2] // 2
    for b in range(gathered.shape[0] // 2):
        one, two = gathered[2 * b], gathered[2 * b + 1]
        top = jnp.concatenate((one[:, :lanes], two[:, :lanes]), axis=1)
        low = jnp.concatenate((one[:, lanes:], two[:, lanes:]), axis=1)
        store(b, jnp.concatenate((top, low), axis=0))


def dot_lanes(a, b):
    return lax.dot_general(a, b, (((1,), (1,)), ((), ())), preferred_element_type=jnp.float32)


def start_kernel(right_ref, message_ref):
    message_ref[...] = pack(right_ref[0], message_ref.shape[0])


def solve_kernel(gathered_ref, inverse_ref, result_ref, message_ref, flat_ref):
    def store(b, block):
        flat_ref[:, b * BS : (b + 1) * BS] = block

    unpack(gathered_ref, store)
    result = dot_lanes(inverse_ref[...], flat_ref[...])
    result_ref[...] = result
    message_ref[...] = pack(result, message_ref.shape[0])


def final_kernel(gathered_ref, inverse_ref, *refs):
    earlier, (out_ref, flat_ref) = refs[:-2], refs[-2:]

    def store(b, block):
        flat_ref[:, b * BS : (b + 1) * BS] = block

    unpack(gathered_ref, store)
    for l, ref in enumerate(earlier):
        out_ref[l] = ref[...]
    out_ref[len(earlier)] = dot_lanes(inverse_ref[...], flat_ref[...])


def update_kernel(tier, last, index_ref, gathered_ref, below_ref, right_ref, *refs):
    earlier = refs[: tier - 1]
    message_ref = refs[tier - 1]
    flat_ref, known_ref = refs[-2], refs[-1]
    base = 0
    for ref in earlier:
        known_ref[base : base + ref.shape[0]] = ref[...]
        base += ref.shape[0]
    first = base

    def store(b, block):
        known_ref[first + b] = block

    unpack(gathered_ref, store)
    if not last:
        kept_ref = refs[tier]
        kept_ref[...] = known_ref[first:]
    for p in range(RB):
        flat_ref[:, p * BS : (p + 1) * BS] = known_ref[index_ref[0, p]]
    groups, _, width = below_ref.shape
    total = right_ref[tier]
    for q in range(groups):
        total = total - dot_lanes(below_ref[q], flat_ref[:, q * width : (q + 1) * width])
    message_ref[...] = pack(total, message_ref.shape[0])


VMEM = pl.BlockSpec(memory_space=pltpu.VMEM)
SMEM = pl.BlockSpec(memory_space=pltpu.SMEM)


def call(kernel, name, outs, scratch, *args, smem=0):
    return pl.pallas_call(
        kernel,
        out_shape=outs,
        in_specs=[SMEM] * smem + [VMEM] * (len(args) - smem),
        out_specs=[VMEM] * len(outs),
        scratch_shapes=scratch,
        cost_estimate=pl.CostEstimate(flops=20_000_000, bytes_accessed=1_000_000, transcendentals=0),
        compiler_params=pltpu.CompilerParams(vmem_limit_bytes=16 * 2**20),
        name=name,
    )(*args)


def on_device(
    right_sides,
    factor_below,
    row_blocks,
    inverse_top,
    inverse_second,
    inverse_third,
    inverse_fourth,
):
    inverses = (inverse_top, inverse_second, inverse_third, inverse_fourth)
    _, rows, columns = right_sides.shape
    devices = lax.axis_size("sn")
    own = lax.axis_index("sn")
    f32, bf16 = jnp.float32, jnp.bfloat16
    shape = jax.ShapeDtypeStruct
    message = (columns // 2, 2 * rows)
    members = [devices >> l for l in range(LEVELS)]

    def gather(copies):
        n = copies.shape[0]
        groups = None
        if n < devices:
            groups = [list(range(s, s + n)) for s in range(0, devices, n)]
        return lax.all_to_all(copies, "sn", 0, 0, axis_index_groups=groups)

    below = [lax.all_gather(factor_below[t], "rhs") for t in range(LEVELS - 1)]
    chosen = lax.dynamic_index_in_dim(row_blocks, own * rows // BS, 1, keepdims=False)
    places = chosen
    base = NB
    for l in range(1, LEVELS - 1):
        count = NB >> l
        mine = own * rows // BS // count * count
        places = jnp.where(chosen // NB == l, chosen - l * NB - mine + base, places)
        base += count

    (copies,) = call(start_kernel, "start", [shape((members[0], *message), bf16)], [], right_sides)
    known = []
    results = []
    for l in range(LEVELS):
        width = members[l] * rows
        gathered = gather(copies)
        flat = pltpu.VMEM((columns, width), bf16)
        if l == LEVELS - 1:
            (out,) = call(
                final_kernel,
                "final",
                [shape((LEVELS, rows, columns), f32)],
                [flat],
                gathered,
                inverses[l],
                *results,
            )
            return out
        result, copies = call(
            solve_kernel,
            f"solve{l}",
            [shape((rows, columns), f32), shape((members[l], *message), bf16)],
            [flat],
            gathered,
            inverses[l],
        )
        results.append(result)
        gathered = gather(copies)
        tier = l + 1
        last = tier == LEVELS - 1
        blocks = sum(NB >> k for k in range(tier))
        outs = [shape((members[tier], *message), bf16)]
        if not last:
            outs.append(shape((NB >> l, columns, BS), bf16))
        got = call(
            functools.partial(update_kernel, tier, last),
            f"update{tier}",
            outs,
            [pltpu.VMEM((columns, RB * BS), bf16), pltpu.VMEM((blocks, columns, BS), bf16)],
            places[l][None],
            gathered,
            below[l],
            right_sides,
            *known,
            smem=1,
        )
        copies = got[0]
        known.extend(got[1:])


def solution(mesh):
    in_specs = (
        P(None, "sn", "rhs"),
        P(None, "sn", "rhs"),
        P(),
        P("sn", None),
        P("sn", None),
        P("sn", None),
        P("sn", None),
    )
    out_specs = P(None, "sn", "rhs")
    return jax.shard_map(
        on_device, mesh=mesh, in_specs=in_specs, out_specs=out_specs, check_vma=False
    )
```

```python
import functools

import jax
import jax.numpy as jnp
from jax import lax
from jax.experimental import pallas as pl
from jax.experimental.pallas import tpu as pltpu
from jax.sharding import PartitionSpec as P

BS = 128
NB = 32
LEVELS = 4
RB = 32


def pack(block, copies):
    half = block.shape[0] // 2
    packed = jnp.concatenate((block[:half], block[half:]), axis=1).astype(jnp.bfloat16)
    return jnp.broadcast_to(packed[None], (copies, *packed.shape))


def unpack(gathered, store):
    lanes = gathered.shape[2] // 2
    for b in range(gathered.shape[0] // 2):
        one, two = gathered[2 * b], gathered[2 * b + 1]
        top = jnp.concatenate((one[:, :lanes], two[:, :lanes]), axis=1)
        low = jnp.concatenate((one[:, lanes:], two[:, lanes:]), axis=1)
        store(b, jnp.concatenate((top, low), axis=0))


def dot_lanes(a, b):
    return lax.dot_general(a, b, (((1,), (1,)), ((), ())), preferred_element_type=jnp.float32)


def start_kernel(right_ref, message_ref):
    message_ref[...] = pack(right_ref[0], message_ref.shape[0])


def solve_kernel(gathered_ref, inverse_ref, result_ref, message_ref, flat_ref):
    def store(b, block):
        flat_ref[:, b * BS : (b + 1) * BS] = block

    unpack(gathered_ref, store)
    result = dot_lanes(flat_ref[...], inverse_ref[...])
    result_ref[...] = result
    message_ref[...] = pack(result, message_ref.shape[0])


def final_kernel(gathered_ref, inverse_ref, *refs):
    earlier, (out_ref, flat_ref) = refs[:-2], refs[-2:]

    def store(b, block):
        flat_ref[:, b * BS : (b + 1) * BS] = block

    unpack(gathered_ref, store)
    for l, ref in enumerate(earlier):
        out_ref[l] = ref[...]
    out_ref[len(earlier)] = dot_lanes(flat_ref[...], inverse_ref[...])


def place(chosen, own_block):
    found, base = chosen, NB
    for l in range(1, LEVELS - 1):
        count = NB >> l
        mine = own_block // count * count
        found = jnp.where(chosen // NB == l, chosen - l * NB - mine + base, found)
        base += count
    return found


def update_kernel(tier, last, parts, index_ref, gathered_ref, right_ref, *refs):
    below, refs = refs[:parts], refs[parts:]
    earlier = refs[: tier - 1]
    message_ref = refs[tier - 1]
    flat_ref, known_ref = refs[-2], refs[-1]
    base = 0
    for ref in earlier:
        known_ref[base : base + ref.shape[0]] = ref[...]
        base += ref.shape[0]
    first = base

    def store(b, block):
        known_ref[first + b] = block

    unpack(gathered_ref, store)
    if not last:
        kept_ref = refs[tier]
        kept_ref[...] = known_ref[first:]
    quarter = RB // parts
    listed = index_ref[tier - 1, RB] + RB
    for k in range(parts):
        first_listed = lax.rem(listed - k * quarter, RB)
        for p in range(quarter):
            at = (k * quarter + p) * BS
            flat_ref[:, at : at + BS] = known_ref[index_ref[tier - 1, first_listed + p]]
    total = right_ref[tier]
    for q, ref in enumerate(below):
        width = ref.shape[1]
        total = total - dot_lanes(flat_ref[:, q * width : (q + 1) * width], ref[...])
    message_ref[...] = pack(total, message_ref.shape[0])


VMEM = pl.BlockSpec(memory_space=pltpu.VMEM)
SMEM = pl.BlockSpec(memory_space=pltpu.SMEM)


def call(kernel, name, outs, scratch, *args, smem=0):
    return pl.pallas_call(
        kernel,
        out_shape=outs,
        in_specs=[SMEM] * smem + [VMEM] * (len(args) - smem),
        out_specs=[VMEM] * len(outs),
        scratch_shapes=scratch,
        cost_estimate=pl.CostEstimate(flops=20_000_000, bytes_accessed=1_000_000, transcendentals=0),
        compiler_params=pltpu.CompilerParams(vmem_limit_bytes=16 * 2**20),
        name=name,
    )(*args)


def on_device(
    right_sides,
    factor_below,
    row_blocks,
    inverse_top,
    inverse_second,
    inverse_third,
    inverse_fourth,
):
    inverses = (inverse_top, inverse_second, inverse_third, inverse_fourth)
    _, rows, columns = right_sides.shape
    right_sides = jnp.swapaxes(right_sides, 1, 2)
    devices = lax.axis_size("sn")
    groups = lax.axis_size("rhs")
    column_group = lax.axis_index("rhs")
    own = lax.axis_index("sn")
    f32, bf16 = jnp.float32, jnp.bfloat16
    shape = jax.ShapeDtypeStruct
    message = (columns // 2, 2 * rows)
    members = [devices >> l for l in range(LEVELS)]

    def gather(copies):
        n = copies.shape[0]
        sets = None
        if n < devices:
            sets = [list(range(s, s + n)) for s in range(0, devices, n)]
        return lax.all_to_all(copies, "sn", 0, 0, axis_index_groups=sets)

    def turn(part):
        got = [part]
        for step in range(1, groups):
            pairs = [(i, (i + step) % groups) for i in range(groups)]
            got.append(lax.ppermute(part, "rhs", pairs))
        return got

    below_first = turn(factor_below[0])
    below_rest = turn(factor_below[1:])
    own_block = own * rows // BS
    chosen = lax.dynamic_index_in_dim(row_blocks, own_block, 1, keepdims=False)
    places = place(chosen, own_block)
    first = jnp.broadcast_to(column_group * (RB // groups), (LEVELS - 1, 1))
    places = jnp.concatenate((places, first), axis=1)
    places, right_sides = lax.optimization_barrier((places, right_sides))
    (copies,) = call(start_kernel, "start", [shape((members[0], *message), bf16)], [], right_sides)
    known = []
    results = []
    for l in range(LEVELS):
        width = members[l] * rows
        gathered = gather(copies)
        flat = pltpu.VMEM((columns, width), bf16)
        if l == LEVELS - 1:
            (out,) = call(
                final_kernel,
                "final",
                [shape((LEVELS, columns, rows), f32)],
                [flat],
                gathered,
                inverses[l],
                *results,
            )
            return jnp.swapaxes(out, 1, 2)
        result, copies = call(
            solve_kernel,
            f"solve{l}",
            [shape((columns, rows), f32), shape((members[l], *message), bf16)],
            [flat],
            gathered,
            inverses[l],
        )
        results.append(result)
        if l == 0:
            copies, *below_first = lax.optimization_barrier((copies, *below_first))
        if l == 1:
            copies, *below_rest = lax.optimization_barrier((copies, *below_rest))
        gathered = gather(copies)
        tier = l + 1
        last = tier == LEVELS - 1
        blocks = sum(NB >> k for k in range(tier))
        outs = [shape((members[tier], *message), bf16)]
        if not last:
            outs.append(shape((NB >> l, columns, BS), bf16))
        got = call(
            functools.partial(update_kernel, tier, last, groups),
            f"update{tier}",
            outs,
            [pltpu.VMEM((columns, RB * BS), bf16), pltpu.VMEM((blocks, columns, BS), bf16)],
            places,
            gathered,
            right_sides,
            *(below_first if l == 0 else [part[l - 1] for part in below_rest]),
            *known,
            smem=1,
        )
        copies = got[0]
        known.extend(got[1:])


def solution(mesh):
    in_specs = (
        P(None, "sn", "rhs"),
        P(None, "sn", "rhs"),
        P(),
        P("sn", None),
        P("sn", None),
        P("sn", None),
        P("sn", None),
    )
    out_specs = P(None, "sn", "rhs")
    return jax.shard_map(
        on_device, mesh=mesh, in_specs=in_specs, out_specs=out_specs, check_vma=False
    )
```

```python
import functools

import jax
import jax.numpy as jnp
from jax import lax
from jax.experimental import pallas as pl
from jax.experimental.pallas import tpu as pltpu
from jax.sharding import PartitionSpec as P

BS = 128
NB = 32
LEVELS = 4
RB = 32


def pack(block, copies):
    half = block.shape[0] // 2
    packed = jnp.concatenate((block[:half], block[half:]), axis=1).astype(jnp.bfloat16)
    return jnp.broadcast_to(packed[None], (copies, *packed.shape))


def unpack(gathered, store):
    lanes = gathered.shape[2] // 2
    for b in range(gathered.shape[0] // 2):
        one, two = gathered[2 * b], gathered[2 * b + 1]
        top = jnp.concatenate((one[:, :lanes], two[:, :lanes]), axis=1)
        low = jnp.concatenate((one[:, lanes:], two[:, lanes:]), axis=1)
        store(b, jnp.concatenate((top, low), axis=0))


def dot_lanes(a, b):
    return lax.dot_general(a, b, (((1,), (1,)), ((), ())), preferred_element_type=jnp.float32)


def start_kernel(right_ref, message_ref):
    message_ref[...] = pack(right_ref[0], message_ref.shape[0])


def solve_kernel(gathered_ref, inverse_ref, result_ref, message_ref, flat_ref):
    def store(b, block):
        flat_ref[:, b * BS : (b + 1) * BS] = block

    unpack(gathered_ref, store)
    result = dot_lanes(flat_ref[...], inverse_ref[...])
    result_ref[...] = result
    message_ref[...] = pack(result, message_ref.shape[0])


def select_kernel(position_ref, *refs):
    below, out_ref = refs[:-1], refs[-1]
    part = below[0].shape[1] // BS
    for j in range(out_ref.shape[2] // BS):
        at = position_ref[0, j]
        for q, ref in enumerate(below):

            @pl.when(at // part == q)
            def _():
                columns = pl.ds(pl.multiple_of(at % part * BS, BS), BS)
                out_ref[0, :, j * BS : (j + 1) * BS] = ref[:, columns]


def join(mine, other, core):
    first = jnp.where(core == 0, mine, other)
    second = jnp.where(core == 0, other, mine)
    return jnp.concatenate((first, second), axis=1)


def final_kernel(
    pieces, gathered_ref, fourth_ref, first_result_ref, second_result_ref, third_ref, third_other_ref, *refs
):
    parent, parent_other = refs[:pieces], refs[pieces : 2 * pieces]
    out_ref, flat_ref, solved_ref, coupled_ref, last_ref = refs[2 * pieces :]
    own = lax.axis_index("sn")
    core, y, z = own % 2, own // 2 % 4, own // 8 % 2
    half = gathered_ref.shape[1] // 2
    devices, rows = gathered_ref.shape[0], fourth_ref.shape[0]

    def store(b, block):
        flat_ref[:, b * BS : (b + 1) * BS] = block

    def store_last(b, block):
        last_ref[:, b * BS : (b + 1) * BS] = block

    def flat(ref):
        return ref[...].reshape(ref.shape[0] * ref.shape[1], ref.shape[2])

    unpack(gathered_ref[:, :half], store)
    in_plane = pl.ds(pl.multiple_of(z * (devices // 2), devices // 2), devices // 2)
    unpack(gathered_ref[in_plane, half:], store_last)
    mine = dot_lanes(flat_ref[...], flat(third_ref))
    other = dot_lanes(flat_ref[...], flat(third_other_ref))
    out_ref[0] = first_result_ref[...]
    out_ref[1] = second_result_ref[...]
    out_ref[2] = mine[:, :rows]
    for e in range(third_ref.shape[0]):
        block = (z ^ (e // 2 % 2)) * pieces + (y ^ (e % 2 * 2 + e // 4))
        at = slice(e * rows, (e + 1) * rows)
        columns = pl.ds(pl.multiple_of(block * BS, BS), BS)
        solved_ref[:, columns] = join(mine[:, at], other[:, at], core).astype(jnp.bfloat16)
    for e in range(pieces):
        mine = dot_lanes(solved_ref[...], parent[e][0])
        other = dot_lanes(solved_ref[...], parent_other[e][0])
        columns = pl.ds(pl.multiple_of((y ^ e) * BS, BS), BS)
        coupled_ref[:, columns] = join(mine, other, core)
    update = last_ref[...].astype(jnp.float32) - coupled_ref[...]
    out_ref[3] = dot_lanes(update.astype(jnp.bfloat16), fourth_ref[...])


def place(chosen, own_block):
    found, base = chosen, NB
    for l in range(1, LEVELS - 1):
        count = NB >> l
        mine = own_block // count * count
        at = chosen - l * NB - mine + base
        if l == LEVELS - 2:
            at = jnp.full_like(chosen, base)
        found = jnp.where(chosen // NB == l, at, found)
        base += count
    return found


def update_kernel(tiers, kept, parts, index_ref, gathered_ref, right_ref, *refs):
    below = [refs[k * parts : (k + 1) * parts] for k in range(len(tiers))]
    refs = refs[len(tiers) * parts :]
    known_ref, flat_ref = refs[-2], refs[-1]
    base = 0
    if not kept:
        base = refs[0].shape[0]
        known_ref[:base] = refs[0][...]
        refs = refs[1:]
    message_ref = refs[0]

    def store(b, block):
        known_ref[base + b] = block

    unpack(gathered_ref, store)
    if kept:
        refs[1][...] = known_ref[...]
    else:
        known_ref[known_ref.shape[0] - 1] = jnp.zeros(known_ref.shape[1:], known_ref.dtype)
    quarter = RB // parts
    slot = 0
    packed = []
    for tier, group in zip(tiers, below):
        listed = index_ref[tier - 1, RB] + RB
        total = right_ref[tier]
        for k, ref in enumerate(group):
            first_listed = lax.rem(listed - k * quarter, RB)
            for p in range(quarter):
                block = known_ref[index_ref[tier - 1, first_listed + p]]
                flat_ref[slot, :, p * BS : (p + 1) * BS] = block
            total = total - dot_lanes(flat_ref[slot], ref[...])
            slot += 1
        packed.append(pack(total, message_ref.shape[0]))
    message_ref[...] = jnp.concatenate(packed, axis=1)


VMEM = pl.BlockSpec(memory_space=pltpu.VMEM)
SMEM = pl.BlockSpec(memory_space=pltpu.SMEM)


def call(kernel, name, outs, scratch, *args, smem=0):
    return pl.pallas_call(
        kernel,
        out_shape=outs,
        in_specs=[SMEM] * smem + [VMEM] * (len(args) - smem),
        out_specs=[VMEM] * len(outs),
        scratch_shapes=scratch,
        cost_estimate=pl.CostEstimate(flops=20_000_000, bytes_accessed=1_000_000, transcendentals=0),
        compiler_params=pltpu.CompilerParams(vmem_limit_bytes=16 * 2**20),
        name=name,
    )(*args)


def on_device(
    right_sides,
    factor_below,
    row_blocks,
    inverse_top,
    inverse_second,
    inverse_third,
    inverse_fourth,
):
    _, rows, columns = right_sides.shape
    right_sides = jnp.swapaxes(right_sides, 1, 2)
    devices = lax.axis_size("sn")
    groups = lax.axis_size("rhs")
    column_group = lax.axis_index("rhs")
    own = lax.axis_index("sn")
    f32, bf16 = jnp.float32, jnp.bfloat16
    shape = jax.ShapeDtypeStruct
    message = (columns // 2, 2 * rows)
    members = [devices >> l for l in range(LEVELS)]
    barrier = lax.optimization_barrier

    def gather(copies):
        n = copies.shape[0]
        sets = None
        if n < devices:
            sets = [list(range(s, s + n)) for s in range(0, devices, n)]
        return lax.all_to_all(copies, "sn", 0, 0, axis_index_groups=sets)

    def turn(part):
        got = [part]
        for step in range(1, groups):
            pairs = [(i, (i + step) % groups) for i in range(groups)]
            got.append(lax.ppermute(part, "rhs", pairs))
        return got

    def swap(part, bit):
        return lax.ppermute(part, "sn", [(i, i ^ bit) for i in range(devices)])

    core, y_low, y_high, z_low = 1, 2, 4, 8

    def over_y(part):
        return [part] + [swap(part, bits) for bits in (y_low, y_high, y_low + y_high)]

    own_block = own * rows // BS
    chosen = lax.dynamic_index_in_dim(row_blocks, own_block, 1, keepdims=False)
    places = place(chosen, own_block)
    first = jnp.broadcast_to(column_group * (RB // groups), (LEVELS - 1, 1))
    places = jnp.concatenate((places, first), axis=1)
    count = NB >> (LEVELS - 2)
    parent = (LEVELS - 2) * NB + own_block // count * count + jnp.arange(count)
    listed = jnp.arange(RB)
    turned = (column_group + groups - listed // (RB // groups)) % groups * (RB // groups)
    turned = turned + listed % (RB // groups)
    hit = chosen[LEVELS - 2][None, :] == parent[:, None]
    positions = jnp.sum(jnp.where(hit, turned[None, :], 0), axis=1)[None].astype(jnp.int32)
    places, positions, right_sides = barrier((places, positions, right_sides))

    first_below = turn(factor_below[0])
    third = inverse_third[None]
    third_got = swap(third, y_high)

    (copies,) = call(start_kernel, "start", [shape((members[0], *message), bf16)], [], right_sides)
    gathered = gather(copies)
    first_result, copies = call(
        solve_kernel,
        "solve0",
        [shape((columns, rows), f32), shape((members[0], *message), bf16)],
        [pltpu.VMEM((columns, members[0] * rows), bf16)],
        gathered,
        inverse_top,
    )

    copies, third_got, *first_below = barrier((copies, third_got, *first_below))
    third = jnp.concatenate((third, third_got))
    third_got = swap(third, z_low)
    rest_below = turn(factor_below[1:])

    gathered = gather(copies)
    copies, known = call(
        functools.partial(update_kernel, (1,), True, groups),
        "update1",
        [shape((members[1], *message), bf16), shape((NB, columns, BS), bf16)],
        [pltpu.VMEM((NB, columns, BS), bf16), pltpu.VMEM((groups, columns, RB // groups * BS), bf16)],
        places,
        gathered,
        right_sides,
        *first_below,
        smem=1,
    )

    copies, third_got = barrier((copies, third_got))
    third = jnp.concatenate((third, third_got))
    third_got = swap(third, y_low)
    second_below = [part[0] for part in rest_below]
    last_below = [part[1] for part in rest_below]
    (coupled,) = call(
        select_kernel, "select", [shape((1, rows, count * BS), bf16)], [], positions, *last_below, smem=1
    )
    coupled = over_y(coupled)

    gathered = gather(copies)
    second_result, copies = call(
        solve_kernel,
        "solve1",
        [shape((columns, rows), f32), shape((members[1], *message), bf16)],
        [pltpu.VMEM((columns, members[1] * rows), bf16)],
        gathered,
        inverse_second,
    )

    gathered = gather(copies)
    blocks = NB + NB // 2 + 1
    (copies,) = call(
        functools.partial(update_kernel, (2, 3), False, groups),
        "update2",
        [shape((members[2], 2 * message[0], message[1]), bf16)],
        [pltpu.VMEM((blocks, columns, BS), bf16), pltpu.VMEM((2 * groups, columns, RB // groups * BS), bf16)],
        places,
        gathered,
        right_sides,
        *second_below,
        *last_below,
        known,
        smem=1,
    )


    copies, coupled, third_got = barrier((copies, coupled, third_got))
    third = jnp.concatenate((third, third_got))
    third_other = swap(third, core)
    coupled_other = [swap(part, core) for part in coupled]

    gathered = gather(copies)
    (out,) = call(
        functools.partial(final_kernel, len(coupled)),
        "final",
        [shape((LEVELS, columns, rows), f32)],
        [
            pltpu.VMEM((columns, members[2] * rows), bf16),
            pltpu.VMEM((columns, members[2] * rows), bf16),
            pltpu.VMEM((columns, members[3] * rows), f32),
            pltpu.VMEM((columns, members[3] * rows), bf16),
        ],
        gathered,
        inverse_fourth,
        first_result,
        second_result,
        third,
        third_other,
        *coupled,
        *coupled_other,
    )
    return jnp.swapaxes(out, 1, 2)


def solution(mesh):
    in_specs = (
        P(None, "sn", "rhs"),
        P(None, "sn", "rhs"),
        P(),
        P("sn", None),
        P("sn", None),
        P("sn", None),
        P("sn", None),
    )
    out_specs = P(None, "sn", "rhs")
    return jax.shard_map(
        on_device, mesh=mesh, in_specs=in_specs, out_specs=out_specs, check_vma=False
    )
```

```python
import functools

import jax
import jax.numpy as jnp
from jax import lax
from jax.experimental import pallas as pl
from jax.experimental.pallas import tpu as pltpu
from jax.sharding import PartitionSpec as P

BS = 128
NB = 32
LEVELS = 4
RB = 32


def pack(block, copies):
    half = block.shape[0] // 2
    packed = jnp.concatenate((block[:half], block[half:]), axis=1).astype(jnp.bfloat16)
    return jnp.broadcast_to(packed[None], (copies, *packed.shape))


def unpack(gathered, store):
    lanes = gathered.shape[2] // 2
    for b in range(gathered.shape[0] // 2):
        one, two = gathered[2 * b], gathered[2 * b + 1]
        top = jnp.concatenate((one[:, :lanes], two[:, :lanes]), axis=1)
        low = jnp.concatenate((one[:, lanes:], two[:, lanes:]), axis=1)
        store(b, jnp.concatenate((top, low), axis=0))


def dot_lanes(a, b):
    return lax.dot_general(a, b, (((1,), (1,)), ((), ())), preferred_element_type=jnp.float32)


def start_kernel(right_ref, message_ref):
    message_ref[...] = pack(right_ref[0], message_ref.shape[0])


def solve_kernel(gathered_ref, inverse_ref, result_ref, message_ref, flat_ref):
    def store(b, block):
        flat_ref[:, b * BS : (b + 1) * BS] = block

    unpack(gathered_ref, store)
    result = dot_lanes(flat_ref[...], inverse_ref[...])
    result_ref[...] = result
    message_ref[...] = pack(result, message_ref.shape[0])


def below_part(near_ref, far_ref, k, tier, tiers):
    ref = near_ref if k < 2 else far_ref
    return ref.at[k % 2 * tiers + tier]


def select_kernel(position_ref, near_ref, far_ref, out_ref):
    positions = position_ref[...]
    part = near_ref.shape[2] // BS
    tiers = near_ref.shape[0] // 2
    for j in range(out_ref.shape[2] // BS):
        at = positions[0, j]
        for k in range(RB // part):

            @pl.when(at // part == k)
            def _():
                columns = pl.ds(pl.multiple_of(at % part * BS, BS), BS)
                block = below_part(near_ref, far_ref, k, tiers - 1, tiers)[:, columns]
                out_ref[0, :, j * BS : (j + 1) * BS] = block


def join(mine, other, core):
    first = jnp.where(core == 0, mine, other)
    second = jnp.where(core == 0, other, mine)
    return jnp.concatenate((first, second), axis=1)


def position():
    own = lax.axis_index("sn")
    return own % 2, own // 2 % 4, own // 8 % 2


def product_kernel(coupled_ref, *refs):
    third, out_ref = refs[:-1], refs[-1]
    core, y, z = position()
    total = None
    for g, ref in enumerate(third):
        picked = []
        for e in range(ref.shape[0]):
            block = (z ^ (e // 2)) * 4 + (y ^ (e % 2 * 2 + g % 2))
            columns = coupled_ref[0, :, pl.ds(pl.multiple_of(block * BS, BS), BS)]
            half = columns.shape[1] // 2
            first = core == g // 2
            picked.append(jnp.where(first, columns[:, :half], columns[:, half:]))
        rows = ref[...].reshape(ref.shape[0] * ref.shape[1], ref.shape[2])
        term = jnp.dot(
            jnp.concatenate(picked, axis=1), rows, preferred_element_type=jnp.float32
        )
        total = term if total is None else total + term
    out_ref[0] = total.astype(out_ref.dtype)


def final_kernel(
    pieces, gathered_ref, third_ref, fourth_ref, first_result_ref, second_result_ref, *refs
):
    parent, parent_other = refs[:pieces], refs[pieces : 2 * pieces]
    out_ref, flat_ref, coupled_ref, last_ref = refs[2 * pieces :]
    core, y, z = position()
    half = gathered_ref.shape[1] // 2
    devices = gathered_ref.shape[0]

    def store(b, block):
        flat_ref[:, b * BS : (b + 1) * BS] = block

    def store_last(b, block):
        last_ref[:, b * BS : (b + 1) * BS] = block

    unpack(gathered_ref[:, :half], store)
    in_plane = pl.ds(pl.multiple_of(z * (devices // 2), devices // 2), devices // 2)
    unpack(gathered_ref[in_plane, half:], store_last)
    out_ref[0] = first_result_ref[...]
    out_ref[1] = second_result_ref[...]
    out_ref[2] = dot_lanes(flat_ref[...], third_ref[...])
    for e in range(pieces):
        mine = dot_lanes(flat_ref[...], parent[e][0])
        other = dot_lanes(flat_ref[...], parent_other[e][0])
        columns = pl.ds(pl.multiple_of((y ^ e) * BS, BS), BS)
        coupled_ref[:, columns] = join(mine, other, core)
    update = last_ref[...].astype(jnp.float32) - coupled_ref[...]
    out_ref[3] = dot_lanes(update.astype(jnp.bfloat16), fourth_ref[...])


def place(chosen, own_block):
    found, base = chosen, NB
    for l in range(1, LEVELS - 1):
        count = NB >> l
        mine = own_block // count * count
        at = chosen - l * NB - mine + base
        if l == LEVELS - 2:
            at = jnp.full_like(chosen, base)
        found = jnp.where(chosen // NB == l, at, found)
        base += count
    return found


def update_kernel(tiers, kept, index_ref, gathered_ref, right_ref, near_ref, far_ref, *refs):
    known_ref, flat_ref = refs[-2], refs[-1]
    base = 0
    if not kept:
        base = refs[0].shape[0]
        known_ref[:base] = refs[0][...]
        refs = refs[1:]
    message_ref = refs[0]

    def store(b, block):
        known_ref[base + b] = block

    unpack(gathered_ref, store)
    if kept:
        refs[1][...] = known_ref[...]
    else:
        known_ref[known_ref.shape[0] - 1] = jnp.zeros(known_ref.shape[1:], known_ref.dtype)
    places = index_ref[...]
    quarter = near_ref.shape[2] // BS
    parts = RB // quarter
    slot = 0
    packed = []
    for t, tier in enumerate(tiers):
        total = right_ref[tier]
        for k in range(parts):
            ref = below_part(near_ref, far_ref, k, t, len(tiers))
            for p in range(quarter):
                block = known_ref[places[tier - 1, k * quarter + p]]
                flat_ref[slot, :, p * BS : (p + 1) * BS] = block
            total = total - dot_lanes(flat_ref[slot], ref[...])
            slot += 1
        packed.append(pack(total, message_ref.shape[0]))
    message_ref[...] = jnp.concatenate(packed, axis=1)


VMEM = pl.BlockSpec(memory_space=pltpu.VMEM)


def held(*arrays):
    return [pltpu.with_memory_space_constraint(array, pltpu.HBM) for array in arrays]


def call(kernel, name, outs, scratch, *args):
    return pl.pallas_call(
        kernel,
        out_shape=outs,
        in_specs=[VMEM] * len(args),
        out_specs=[VMEM] * len(outs),
        scratch_shapes=scratch,
        cost_estimate=pl.CostEstimate(flops=20_000_000, bytes_accessed=1_000_000, transcendentals=0),
        compiler_params=pltpu.CompilerParams(vmem_limit_bytes=16 * 2**20),
        name=name,
    )(*args)


def on_device(
    right_sides,
    factor_below,
    row_blocks,
    inverse_top,
    inverse_second,
    inverse_third,
    inverse_fourth,
):
    _, rows, columns = right_sides.shape
    right_sides = jnp.swapaxes(right_sides, 1, 2)
    devices = lax.axis_size("sn")
    groups = lax.axis_size("rhs")
    column_group = lax.axis_index("rhs")
    own = lax.axis_index("sn")
    f32, bf16 = jnp.float32, jnp.bfloat16
    shape = jax.ShapeDtypeStruct
    message = (columns // 2, 2 * rows)
    members = [devices >> l for l in range(LEVELS)]
    barrier = lax.optimization_barrier

    def gather(copies):
        n = copies.shape[0]
        sets = None
        if n < devices:
            sets = [list(range(s, s + n)) for s in range(0, devices, n)]
        return lax.all_to_all(copies, "sn", 0, 0, axis_index_groups=sets)

    def swap_group(part, bit):
        return lax.ppermute(part, "rhs", [(i, i ^ bit) for i in range(groups)])

    def swap(part, bit):
        return lax.ppermute(part, "sn", [(i, i ^ bit) for i in range(devices)])

    core, y_low, y_high, z_low = 1, 2, 4, 8

    def over_y(part):
        return [part] + [swap(part, bits) for bits in (y_low, y_high, y_low + y_high)]

    own_block = own * rows // BS
    chosen = lax.dynamic_index_in_dim(row_blocks, own_block, 1, keepdims=False)
    places = place(chosen, own_block)
    quarter = RB // groups
    part = jnp.arange(groups)
    source = (column_group ^ part)[:, None] == part[None, :]
    listed = places.reshape(LEVELS - 1, 1, groups, quarter)
    places = jnp.sum(jnp.where(source[None, :, :, None], listed, 0), axis=2)
    places = places.reshape(LEVELS - 1, RB)
    count = NB >> (LEVELS - 2)
    parent = (LEVELS - 2) * NB + own_block // count * count + jnp.arange(count)
    listed = jnp.arange(RB)
    turned = (column_group ^ listed // quarter) * quarter + listed % quarter
    hit = chosen[LEVELS - 2][None, :] == parent[:, None]
    positions = jnp.sum(jnp.where(hit, turned[None, :], 0), axis=1)[None].astype(jnp.int32)
    places, positions, right_sides = barrier((places, positions, right_sides))

    below = factor_below
    below_got = swap_group(below, 1)
    third = inverse_third[None]
    third_got = [swap(third, bits) for bits in (y_high, z_low, y_high + z_low)]

    (copies,) = call(start_kernel, "start", [shape((members[0], *message), bf16)], [], right_sides)
    gathered = gather(copies)
    first_result, copies = call(
        solve_kernel,
        "solve0",
        [shape((columns, rows), f32), shape((members[0], *message), bf16)],
        [pltpu.VMEM((columns, members[0] * rows), bf16)],
        gathered,
        inverse_top,
    )

    copies, third_got, below_got = barrier((copies, third_got, below_got))
    first_below = jnp.stack((below[0], below_got[0]))
    first_far = swap_group(first_below, 2)
    rest_below = jnp.concatenate((below[1:], below_got[1:]))
    rest_far = swap_group(rest_below, 2)
    third = jnp.concatenate((third, *third_got))
    third_got = swap(third, y_low)

    gathered = gather(copies)
    copies, known = call(
        functools.partial(update_kernel, (1,), True),
        "update1",
        [shape((members[1], *message), bf16), shape((NB, columns, BS), bf16)],
        [pltpu.VMEM((NB, columns, BS), bf16), pltpu.VMEM((groups, columns, RB // groups * BS), bf16)],
        places,
        gathered,
        right_sides,
        first_below,
        first_far,
    )

    copies, third_got = barrier((copies, third_got))
    third = [third, third_got]
    third = third + [swap(part, core) for part in third]
    (coupled,) = call(
        select_kernel, "select", [shape((1, rows, count * BS), bf16)], [], positions, rest_below, rest_far
    )

    gathered = gather(copies)
    second_result, copies = call(
        solve_kernel,
        "solve1",
        [shape((columns, rows), f32), shape((members[1], *message), bf16)],
        [pltpu.VMEM((columns, members[1] * rows), bf16)],
        gathered,
        inverse_second,
    )

    copies, coupled, third = barrier((copies, coupled, third))
    (coupled,) = call(
        product_kernel, "product", [shape(coupled.shape, bf16)], [], coupled, *held(*third)
    )
    coupled = over_y(coupled)

    gathered = gather(copies)
    blocks = NB + NB // 2 + 1
    (copies,) = call(
        functools.partial(update_kernel, (2, 3), False),
        "update2",
        [shape((members[2], 2 * message[0], message[1]), bf16)],
        [pltpu.VMEM((blocks, columns, BS), bf16), pltpu.VMEM((2 * groups, columns, RB // groups * BS), bf16)],
        places,
        gathered,
        right_sides,
        rest_below,
        rest_far,
        known,
    )

    coupled_other = [swap(part, core) for part in coupled]

    gathered = gather(copies)
    (out,) = call(
        functools.partial(final_kernel, len(coupled)),
        "final",
        [shape((LEVELS, columns, rows), f32)],
        [
            pltpu.VMEM((columns, members[2] * rows), bf16),
            pltpu.VMEM((columns, members[3] * rows), f32),
            pltpu.VMEM((columns, members[3] * rows), bf16),
        ],
        gathered,
        inverse_third,
        inverse_fourth,
        first_result,
        second_result,
        *coupled,
        *coupled_other,
    )
    return jnp.swapaxes(out, 1, 2)


def solution(mesh):
    in_specs = (
        P(None, "sn", "rhs"),
        P(None, "sn", "rhs"),
        P(),
        P("sn", None),
        P("sn", None),
        P("sn", None),
        P("sn", None),
    )
    out_specs = P(None, "sn", "rhs")
    return jax.shard_map(
        on_device, mesh=mesh, in_specs=in_specs, out_specs=out_specs, check_vma=False
    )
```

```python
import functools

import jax
import jax.numpy as jnp
from jax import lax
from jax.experimental import pallas as pl
from jax.experimental.pallas import tpu as pltpu
from jax.sharding import PartitionSpec as P

BS = 128
NB = 32
LEVELS = 4
RB = 32


def pack(block, copies):
    half = block.shape[0] // 2
    packed = jnp.concatenate((block[:half], block[half:]), axis=1).astype(jnp.bfloat16)
    return jnp.broadcast_to(packed[None], (copies, *packed.shape))


def unpack(gathered, store):
    lanes = gathered.shape[2] // 2
    for b in range(gathered.shape[0] // 2):
        one, two = gathered[2 * b], gathered[2 * b + 1]
        top = jnp.concatenate((one[:, :lanes], two[:, :lanes]), axis=1)
        low = jnp.concatenate((one[:, lanes:], two[:, lanes:]), axis=1)
        store(b, jnp.concatenate((top, low), axis=0))


def dot_lanes(a, b):
    return lax.dot_general(a, b, (((1,), (1,)), ((), ())), preferred_element_type=jnp.float32)


def start_kernel(right_ref, message_ref):
    message_ref[...] = pack(right_ref[0], message_ref.shape[0])


def solve_kernel(gathered_ref, inverse_ref, result_ref, message_ref, flat_ref):
    def store(b, block):
        flat_ref[:, b * BS : (b + 1) * BS] = block

    unpack(gathered_ref, store)
    result = dot_lanes(flat_ref[...], inverse_ref[...])
    result_ref[...] = result
    message_ref[...] = pack(result, message_ref.shape[0])


def below_part(near_ref, far_ref, k, tier, tiers):
    ref = near_ref if k < 2 else far_ref
    return ref.at[k % 2 * tiers + tier]


def select_kernel(position_ref, near_ref, far_ref, out_ref):
    positions = position_ref[...]
    part = near_ref.shape[2] // BS
    tiers = near_ref.shape[0] // 2
    for j in range(out_ref.shape[2] // BS):
        at = positions[0, j]
        for k in range(RB // part):

            @pl.when(at // part == k)
            def _():
                columns = pl.ds(pl.multiple_of(at % part * BS, BS), BS)
                block = below_part(near_ref, far_ref, k, tiers - 1, tiers)[:, columns]
                out_ref[0, :, j * BS : (j + 1) * BS] = block


def join(mine, other, core):
    first = jnp.where(core == 0, mine, other)
    second = jnp.where(core == 0, other, mine)
    return jnp.concatenate((first, second), axis=1)


def position():
    own = lax.axis_index("sn")
    return own % 2, own // 2 % 4, own // 8 % 2


def product_kernel(coupled_ref, *refs):
    third, out_ref = refs[:-1], refs[-1]
    core, y, z = position()
    total = None
    for n, ref in enumerate(third):
        g = n % 4
        picked = []
        for e in range(ref.shape[0]) if n < 4 else (3,):
            block = (z ^ (e // 2)) * 4 + (y ^ (e % 2 * 2 + g % 2))
            columns = coupled_ref[0, :, pl.ds(pl.multiple_of(block * BS, BS), BS)]
            half = columns.shape[1] // 2
            first = core == g // 2
            picked.append(jnp.where(first, columns[:, :half], columns[:, half:]))
        rows = ref[...].reshape(ref.shape[0] * ref.shape[1], ref.shape[2])
        term = jnp.dot(
            jnp.concatenate(picked, axis=1), rows, preferred_element_type=jnp.float32
        )
        total = term if total is None else total + term
    out_ref[0] = total.astype(out_ref.dtype)


def final_kernel(
    pieces, gathered_ref, third_ref, fourth_ref, first_result_ref, second_result_ref, *refs
):
    parent, parent_other = refs[:pieces], refs[pieces : 2 * pieces]
    out_ref, flat_ref, coupled_ref, last_ref = refs[2 * pieces :]
    core, y, z = position()
    half = gathered_ref.shape[1] // 2
    devices = gathered_ref.shape[0]

    def store(b, block):
        flat_ref[:, b * BS : (b + 1) * BS] = block

    def store_last(b, block):
        last_ref[:, b * BS : (b + 1) * BS] = block

    unpack(gathered_ref[:, :half], store)
    in_plane = pl.ds(pl.multiple_of(z * (devices // 2), devices // 2), devices // 2)
    unpack(gathered_ref[in_plane, half:], store_last)
    out_ref[0] = first_result_ref[...]
    out_ref[1] = second_result_ref[...]
    out_ref[2] = dot_lanes(flat_ref[...], third_ref[...])
    for e in range(pieces):
        mine = dot_lanes(flat_ref[...], parent[e][0])
        other = dot_lanes(flat_ref[...], parent_other[e][0])
        columns = pl.ds(pl.multiple_of((y ^ e) * BS, BS), BS)
        coupled_ref[:, columns] = join(mine, other, core)
    update = last_ref[...].astype(jnp.float32) - coupled_ref[...]
    out_ref[3] = dot_lanes(update.astype(jnp.bfloat16), fourth_ref[...])


def place(chosen, own_block):
    found, base = chosen, NB
    for l in range(1, LEVELS - 1):
        count = NB >> l
        mine = own_block // count * count
        at = chosen - l * NB - mine + base
        if l == LEVELS - 2:
            at = jnp.full_like(chosen, base)
        found = jnp.where(chosen // NB == l, at, found)
        base += count
    return found


def update_kernel(tiers, kept, index_ref, gathered_ref, right_ref, near_ref, far_ref, *refs):
    known_ref, flat_ref = refs[-2], refs[-1]
    base = 0
    if not kept:
        base = refs[0].shape[0]
        known_ref[:base] = refs[0][...]
        refs = refs[1:]
    message_ref = refs[0]

    def store(b, block):
        known_ref[base + b] = block

    unpack(gathered_ref, store)
    if kept:
        refs[1][...] = known_ref[...]
    else:
        known_ref[known_ref.shape[0] - 1] = jnp.zeros(known_ref.shape[1:], known_ref.dtype)
    places = index_ref[...]
    quarter = near_ref.shape[2] // BS
    parts = RB // quarter
    slot = 0
    packed = []
    for t, tier in enumerate(tiers):
        total = right_ref[tier]
        for k in range(parts):
            ref = below_part(near_ref, far_ref, k, t, len(tiers))
            for p in range(quarter):
                block = known_ref[places[tier - 1, k * quarter + p]]
                flat_ref[slot, :, p * BS : (p + 1) * BS] = block
            total = total - dot_lanes(flat_ref[slot], ref[...])
            slot += 1
        packed.append(pack(total, message_ref.shape[0]))
    message_ref[...] = jnp.concatenate(packed, axis=1)


VMEM = pl.BlockSpec(memory_space=pltpu.VMEM)


def held(*arrays):
    return [pltpu.with_memory_space_constraint(array, pltpu.HBM) for array in arrays]


def call(kernel, name, outs, scratch, *args):
    return pl.pallas_call(
        kernel,
        out_shape=outs,
        in_specs=[VMEM] * len(args),
        out_specs=[VMEM] * len(outs),
        scratch_shapes=scratch,
        cost_estimate=pl.CostEstimate(flops=20_000_000, bytes_accessed=1_000_000, transcendentals=0),
        compiler_params=pltpu.CompilerParams(vmem_limit_bytes=16 * 2**20),
        name=name,
    )(*args)


def on_device(
    right_sides,
    factor_below,
    row_blocks,
    inverse_top,
    inverse_second,
    inverse_third,
    inverse_fourth,
):
    _, rows, columns = right_sides.shape
    right_sides = jnp.swapaxes(right_sides, 1, 2)
    devices = lax.axis_size("sn")
    groups = lax.axis_size("rhs")
    column_group = lax.axis_index("rhs")
    own = lax.axis_index("sn")
    f32, bf16 = jnp.float32, jnp.bfloat16
    shape = jax.ShapeDtypeStruct
    message = (columns // 2, 2 * rows)
    members = [devices >> l for l in range(LEVELS)]
    barrier = lax.optimization_barrier

    def gather(copies):
        n = copies.shape[0]
        sets = None
        if n < devices:
            sets = [list(range(s, s + n)) for s in range(0, devices, n)]
        return lax.all_to_all(copies, "sn", 0, 0, axis_index_groups=sets)

    def swap_group(part, bit):
        return lax.ppermute(part, "rhs", [(i, i ^ bit) for i in range(groups)])

    def swap(part, bit):
        return lax.ppermute(part, "sn", [(i, i ^ bit) for i in range(devices)])

    core, y_low, y_high, z_low = 1, 2, 4, 8

    def over_y(part):
        return [part] + [swap(part, bits) for bits in (y_low, y_high, y_low + y_high)]

    own_block = own * rows // BS
    chosen = lax.dynamic_index_in_dim(row_blocks, own_block, 1, keepdims=False)
    places = place(chosen, own_block)
    quarter = RB // groups
    part = jnp.arange(groups)
    source = (column_group ^ part)[:, None] == part[None, :]
    listed = places.reshape(LEVELS - 1, 1, groups, quarter)
    places = jnp.sum(jnp.where(source[None, :, :, None], listed, 0), axis=2)
    places = places.reshape(LEVELS - 1, RB)
    count = NB >> (LEVELS - 2)
    parent = (LEVELS - 2) * NB + own_block // count * count + jnp.arange(count)
    listed = jnp.arange(RB)
    turned = (column_group ^ listed // quarter) * quarter + listed % quarter
    hit = chosen[LEVELS - 2][None, :] == parent[:, None]
    positions = jnp.sum(jnp.where(hit, turned[None, :], 0), axis=1)[None].astype(jnp.int32)
    places, positions, right_sides = barrier((places, positions, right_sides))

    below = factor_below
    below_got = swap_group(below, 1)
    third = inverse_third[None]
    far, near = swap(third, y_high), swap(third, z_low)

    (copies,) = call(start_kernel, "start", [shape((members[0], *message), bf16)], [], right_sides)
    gathered = gather(copies)
    first_result, copies = call(
        solve_kernel,
        "solve0",
        [shape((columns, rows), f32), shape((members[0], *message), bf16)],
        [pltpu.VMEM((columns, members[0] * rows), bf16)],
        gathered,
        inverse_top,
    )

    copies, (far, near), below_got = barrier((copies, (far, near), below_got))
    first_below = jnp.stack((below[0], below_got[0]))
    first_far = swap_group(first_below, 2)
    rest_below = jnp.concatenate((below[1:], below_got[1:]))
    rest_far = swap_group(rest_below, 2)
    third = jnp.concatenate((third, far, near))
    third_got = swap(third, y_low)
    corner = swap(far, z_low)

    gathered = gather(copies)
    copies, known = call(
        functools.partial(update_kernel, (1,), True),
        "update1",
        [shape((members[1], *message), bf16), shape((NB, columns, BS), bf16)],
        [pltpu.VMEM((NB, columns, BS), bf16), pltpu.VMEM((groups, columns, RB // groups * BS), bf16)],
        places,
        gathered,
        right_sides,
        first_below,
        first_far,
    )

    copies, third_got, corner = barrier((copies, third_got, corner))
    corner = [corner, swap(corner, y_low)]
    third = [third, third_got]
    third = third + [swap(part, core) for part in third]
    corner = corner + [swap(part, core) for part in corner]
    (coupled,) = call(
        select_kernel, "select", [shape((1, rows, count * BS), bf16)], [], positions, rest_below, rest_far
    )

    gathered = gather(copies)
    second_result, copies = call(
        solve_kernel,
        "solve1",
        [shape((columns, rows), f32), shape((members[1], *message), bf16)],
        [pltpu.VMEM((columns, members[1] * rows), bf16)],
        gathered,
        inverse_second,
    )

    copies, coupled, third = barrier((copies, coupled, third))
    third = third + corner
    (coupled,) = call(
        product_kernel, "product", [shape(coupled.shape, bf16)], [], coupled, *held(*third[:4]), *third[4:]
    )
    coupled = over_y(coupled)

    gathered = gather(copies)
    blocks = NB + NB // 2 + 1
    (copies,) = call(
        functools.partial(update_kernel, (2, 3), False),
        "update2",
        [shape((members[2], 2 * message[0], message[1]), bf16)],
        [pltpu.VMEM((blocks, columns, BS), bf16), pltpu.VMEM((2 * groups, columns, RB // groups * BS), bf16)],
        places,
        gathered,
        right_sides,
        rest_below,
        rest_far,
        known,
    )

    coupled_other = [swap(part, core) for part in coupled]

    gathered = gather(copies)
    (out,) = call(
        functools.partial(final_kernel, len(coupled)),
        "final",
        [shape((LEVELS, columns, rows), f32)],
        [
            pltpu.VMEM((columns, members[2] * rows), bf16),
            pltpu.VMEM((columns, members[3] * rows), f32),
            pltpu.VMEM((columns, members[3] * rows), bf16),
        ],
        gathered,
        inverse_third,
        inverse_fourth,
        first_result,
        second_result,
        *coupled,
        *coupled_other,
    )
    return jnp.swapaxes(out, 1, 2)


def solution(mesh):
    in_specs = (
        P(None, "sn", "rhs"),
        P(None, "sn", "rhs"),
        P(),
        P("sn", None),
        P("sn", None),
        P("sn", None),
        P("sn", None),
    )
    out_specs = P(None, "sn", "rhs")
    return jax.shard_map(
        on_device, mesh=mesh, in_specs=in_specs, out_specs=out_specs, check_vma=False
    )
```

```python
import functools

import jax
import jax.numpy as jnp
from jax import lax
from jax.experimental import pallas as pl
from jax.experimental.pallas import tpu as pltpu
from jax.sharding import PartitionSpec as P

BS = 128
NB = 32
LEVELS = 4
RB = 32


def pack(block, copies):
    half = block.shape[0] // 2
    packed = jnp.concatenate((block[:half], block[half:]), axis=1).astype(jnp.bfloat16)
    return jnp.broadcast_to(packed[None], (copies, *packed.shape))


def unpack(gathered, store):
    lanes = gathered.shape[2] // 2
    for b in range(gathered.shape[0] // 2):
        one, two = gathered[2 * b], gathered[2 * b + 1]
        top = jnp.concatenate((one[:, :lanes], two[:, :lanes]), axis=1)
        low = jnp.concatenate((one[:, lanes:], two[:, lanes:]), axis=1)
        store(b, jnp.concatenate((top, low), axis=0))


def dot_lanes(a, b):
    return lax.dot_general(a, b, (((1,), (1,)), ((), ())), preferred_element_type=jnp.float32)


def start_kernel(right_ref, message_ref):
    message_ref[...] = pack(right_ref[0], message_ref.shape[0])


def solve_kernel(gathered_ref, inverse_ref, result_ref, message_ref, flat_ref):
    def store(b, block):
        flat_ref[:, b * BS : (b + 1) * BS] = block

    unpack(gathered_ref, store)
    result = dot_lanes(flat_ref[...], inverse_ref[...])
    result_ref[...] = result
    message_ref[...] = pack(result, message_ref.shape[0])


def below_part(near_ref, far_ref, k, tier, tiers):
    ref = near_ref if k < 2 else far_ref
    return ref.at[k % 2 * tiers + tier]


def select_kernel(position_ref, near_ref, far_ref, out_ref):
    positions = position_ref[...]
    part = near_ref.shape[2] // BS
    tiers = near_ref.shape[0] // 2
    for j in range(out_ref.shape[2] // BS):
        at = positions[0, j]
        for k in range(RB // part):

            @pl.when(at // part == k)
            def _():
                columns = pl.ds(pl.multiple_of(at % part * BS, BS), BS)
                block = below_part(near_ref, far_ref, k, tiers - 1, tiers)[:, columns]
                out_ref[0, :, j * BS : (j + 1) * BS] = block


def join(mine, other, core):
    first = jnp.where(core == 0, mine, other)
    second = jnp.where(core == 0, other, mine)
    return jnp.concatenate((first, second), axis=1)


def position():
    own = lax.axis_index("sn")
    return own % 2, own // 2 % 4, own // 8 % 2


def product_kernel(corner, coupled_ref, *refs):
    third, out_ref = refs[:4], refs[-1]
    core, y, z = position()
    total = refs[4][0] if corner else None
    for g, ref in enumerate(third):
        picked = []
        for e in (3,) if corner else range(ref.shape[0]):
            block = (z ^ (e // 2)) * 4 + (y ^ (e % 2 * 2 + g % 2))
            columns = coupled_ref[0, :, pl.ds(pl.multiple_of(block * BS, BS), BS)]
            half = columns.shape[1] // 2
            first = core == g // 2
            picked.append(jnp.where(first, columns[:, :half], columns[:, half:]))
        rows = ref[...].reshape(ref.shape[0] * ref.shape[1], ref.shape[2])
        picked = picked[0] if corner else jnp.concatenate(picked, axis=1)
        term = jnp.dot(picked, rows, preferred_element_type=jnp.float32)
        total = term if total is None else total + term
    out_ref[0] = total.astype(out_ref.dtype)


def final_kernel(
    pieces, gathered_ref, third_ref, fourth_ref, first_result_ref, second_result_ref, *refs
):
    parent, parent_other = refs[:pieces], refs[pieces : 2 * pieces]
    out_ref, flat_ref, coupled_ref, last_ref = refs[2 * pieces :]
    core, y, z = position()
    half = gathered_ref.shape[1] // 2
    devices = gathered_ref.shape[0]

    def store(b, block):
        flat_ref[:, b * BS : (b + 1) * BS] = block

    def store_last(b, block):
        last_ref[:, b * BS : (b + 1) * BS] = block

    unpack(gathered_ref[:, :half], store)
    in_plane = pl.ds(pl.multiple_of(z * (devices // 2), devices // 2), devices // 2)
    unpack(gathered_ref[in_plane, half:], store_last)
    out_ref[0] = first_result_ref[...]
    out_ref[1] = second_result_ref[...]
    out_ref[2] = dot_lanes(flat_ref[...], third_ref[...])
    for e in range(pieces):
        mine = dot_lanes(flat_ref[...], parent[e][0])
        other = dot_lanes(flat_ref[...], parent_other[e][0])
        columns = pl.ds(pl.multiple_of((y ^ e) * BS, BS), BS)
        coupled_ref[:, columns] = join(mine, other, core)
    update = last_ref[...].astype(jnp.float32) - coupled_ref[...]
    out_ref[3] = dot_lanes(update.astype(jnp.bfloat16), fourth_ref[...])


def place(chosen, own_block):
    found, base = chosen, NB
    for l in range(1, LEVELS - 1):
        count = NB >> l
        mine = own_block // count * count
        at = chosen - l * NB - mine + base
        if l == LEVELS - 2:
            at = jnp.full_like(chosen, base)
        found = jnp.where(chosen // NB == l, at, found)
        base += count
    return found


def update_kernel(tiers, kept, index_ref, gathered_ref, right_ref, near_ref, far_ref, *refs):
    known_ref, flat_ref = refs[-2], refs[-1]
    base = 0
    if not kept:
        base = refs[0].shape[0]
        known_ref[:base] = refs[0][...]
        refs = refs[1:]
    message_ref = refs[0]

    def store(b, block):
        known_ref[base + b] = block

    unpack(gathered_ref, store)
    if kept:
        refs[1][...] = known_ref[...]
    else:
        known_ref[known_ref.shape[0] - 1] = jnp.zeros(known_ref.shape[1:], known_ref.dtype)
    places = index_ref[...]
    quarter = near_ref.shape[2] // BS
    parts = RB // quarter
    slot = 0
    packed = []
    for t, tier in enumerate(tiers):
        total = right_ref[tier]
        for k in range(parts):
            ref = below_part(near_ref, far_ref, k, t, len(tiers))
            for p in range(quarter):
                block = known_ref[places[tier - 1, k * quarter + p]]
                flat_ref[slot, :, p * BS : (p + 1) * BS] = block
            total = total - dot_lanes(flat_ref[slot], ref[...])
            slot += 1
        packed.append(pack(total, message_ref.shape[0]))
    message_ref[...] = jnp.concatenate(packed, axis=1)


VMEM = pl.BlockSpec(memory_space=pltpu.VMEM)


def held(*arrays):
    return [pltpu.with_memory_space_constraint(array, pltpu.HBM) for array in arrays]


def call(kernel, name, outs, scratch, *args):
    return pl.pallas_call(
        kernel,
        out_shape=outs,
        in_specs=[VMEM] * len(args),
        out_specs=[VMEM] * len(outs),
        scratch_shapes=scratch,
        cost_estimate=pl.CostEstimate(flops=20_000_000, bytes_accessed=1_000_000, transcendentals=0),
        compiler_params=pltpu.CompilerParams(vmem_limit_bytes=16 * 2**20),
        name=name,
    )(*args)


def on_device(
    right_sides,
    factor_below,
    row_blocks,
    inverse_top,
    inverse_second,
    inverse_third,
    inverse_fourth,
):
    _, rows, columns = right_sides.shape
    right_sides = jnp.swapaxes(right_sides, 1, 2)
    devices = lax.axis_size("sn")
    groups = lax.axis_size("rhs")
    column_group = lax.axis_index("rhs")
    own = lax.axis_index("sn")
    f32, bf16 = jnp.float32, jnp.bfloat16
    shape = jax.ShapeDtypeStruct
    message = (columns // 2, 2 * rows)
    members = [devices >> l for l in range(LEVELS)]
    barrier = lax.optimization_barrier

    def gather(copies):
        n = copies.shape[0]
        sets = None
        if n < devices:
            sets = [list(range(s, s + n)) for s in range(0, devices, n)]
        return lax.all_to_all(copies, "sn", 0, 0, axis_index_groups=sets)

    def swap_group(part, bit):
        return lax.ppermute(part, "rhs", [(i, i ^ bit) for i in range(groups)])

    def swap(part, bit):
        return lax.ppermute(part, "sn", [(i, i ^ bit) for i in range(devices)])

    core, y_low, y_high, z_low = 1, 2, 4, 8

    def over_y(part):
        return [part] + [swap(part, bits) for bits in (y_low, y_high, y_low + y_high)]

    own_block = own * rows // BS
    chosen = lax.dynamic_index_in_dim(row_blocks, own_block, 1, keepdims=False)
    places = place(chosen, own_block)
    quarter = RB // groups
    part = jnp.arange(groups)
    source = (column_group ^ part)[:, None] == part[None, :]
    listed = places.reshape(LEVELS - 1, 1, groups, quarter)
    places = jnp.sum(jnp.where(source[None, :, :, None], listed, 0), axis=2)
    places = places.reshape(LEVELS - 1, RB)
    count = NB >> (LEVELS - 2)
    parent = (LEVELS - 2) * NB + own_block // count * count + jnp.arange(count)
    listed = jnp.arange(RB)
    turned = (column_group ^ listed // quarter) * quarter + listed % quarter
    hit = chosen[LEVELS - 2][None, :] == parent[:, None]
    positions = jnp.sum(jnp.where(hit, turned[None, :], 0), axis=1)[None].astype(jnp.int32)
    places, positions, right_sides = barrier((places, positions, right_sides))

    below = factor_below
    below_got = swap_group(below, 1)
    third = inverse_third[None]
    far, near = swap(third, y_high), swap(third, z_low)

    (copies,) = call(start_kernel, "start", [shape((members[0], *message), bf16)], [], right_sides)
    gathered = gather(copies)
    first_result, copies = call(
        solve_kernel,
        "solve0",
        [shape((columns, rows), f32), shape((members[0], *message), bf16)],
        [pltpu.VMEM((columns, members[0] * rows), bf16)],
        gathered,
        inverse_top,
    )

    copies, (far, near), below_got = barrier((copies, (far, near), below_got))
    first_below = jnp.stack((below[0], below_got[0]))
    first_far = swap_group(first_below, 2)
    rest_below = jnp.concatenate((below[1:], below_got[1:]))
    rest_far = swap_group(rest_below, 2)
    third = jnp.concatenate((third, far, near))
    third_got = swap(third, y_low)
    corner = swap(far, z_low)

    gathered = gather(copies)
    copies, known = call(
        functools.partial(update_kernel, (1,), True),
        "update1",
        [shape((members[1], *message), bf16), shape((NB, columns, BS), bf16)],
        [pltpu.VMEM((NB, columns, BS), bf16), pltpu.VMEM((groups, columns, RB // groups * BS), bf16)],
        places,
        gathered,
        right_sides,
        first_below,
        first_far,
    )

    copies, third_got, corner = barrier((copies, third_got, corner))
    corner = [corner, swap(corner, y_low)]
    third = [third, third_got]
    third = third + [swap(part, core) for part in third]
    corner = corner + [swap(part, core) for part in corner]
    (coupled,) = call(
        select_kernel, "select", [shape((1, rows, count * BS), bf16)], [], positions, rest_below, rest_far
    )

    (partial,) = call(
        functools.partial(product_kernel, False),
        "product",
        [shape(coupled.shape, f32)],
        [],
        coupled,
        *held(*third),
    )
    gathered = gather(copies)
    gathered, coupled, partial = barrier((gathered, coupled, partial))
    second_result, copies = call(
        solve_kernel,
        "solve1",
        [shape((columns, rows), f32), shape((members[1], *message), bf16)],
        [pltpu.VMEM((columns, members[1] * rows), bf16)],
        gathered,
        inverse_second,
    )

    (coupled,) = call(
        functools.partial(product_kernel, True),
        "corner",
        [shape(coupled.shape, bf16)],
        [],
        coupled,
        *corner,
        partial,
    )
    coupled = over_y(coupled)

    gathered = gather(copies)
    blocks = NB + NB // 2 + 1
    (copies,) = call(
        functools.partial(update_kernel, (2, 3), False),
        "update2",
        [shape((members[2], 2 * message[0], message[1]), bf16)],
        [pltpu.VMEM((blocks, columns, BS), bf16), pltpu.VMEM((2 * groups, columns, RB // groups * BS), bf16)],
        places,
        gathered,
        right_sides,
        rest_below,
        rest_far,
        known,
    )

    coupled_other = [swap(part, core) for part in coupled]

    gathered = gather(copies)
    (out,) = call(
        functools.partial(final_kernel, len(coupled)),
        "final",
        [shape((LEVELS, columns, rows), f32)],
        [
            pltpu.VMEM((columns, members[2] * rows), bf16),
            pltpu.VMEM((columns, members[3] * rows), f32),
            pltpu.VMEM((columns, members[3] * rows), bf16),
        ],
        gathered,
        inverse_third,
        inverse_fourth,
        first_result,
        second_result,
        *coupled,
        *coupled_other,
    )
    return jnp.swapaxes(out, 1, 2)


def solution(mesh):
    in_specs = (
        P(None, "sn", "rhs"),
        P(None, "sn", "rhs"),
        P(),
        P("sn", None),
        P("sn", None),
        P("sn", None),
        P("sn", None),
    )
    out_specs = P(None, "sn", "rhs")
    return jax.shard_map(
        on_device, mesh=mesh, in_specs=in_specs, out_specs=out_specs, check_vma=False
    )
```

```python
import functools

import jax
import jax.numpy as jnp
from jax import lax
from jax.experimental import pallas as pl
from jax.experimental.pallas import tpu as pltpu
from jax.sharding import PartitionSpec as P

BS = 128
NB = 32
LEVELS = 4
RB = 32


def pack(block, copies):
    half = block.shape[0] // 2
    packed = jnp.concatenate((block[:half], block[half:]), axis=1).astype(jnp.bfloat16)
    return jnp.broadcast_to(packed[None], (copies, *packed.shape))


def unpack_cores(mine_ref, other_ref, store):
    core = lax.axis_index("sn") % 2
    lanes = mine_ref.shape[2] // 2
    for b in range(mine_ref.shape[0]):
        one = jnp.where(core == 0, mine_ref[b], other_ref[b])
        two = jnp.where(core == 0, other_ref[b], mine_ref[b])
        top = jnp.concatenate((one[:, :lanes], two[:, :lanes]), axis=1)
        low = jnp.concatenate((one[:, lanes:], two[:, lanes:]), axis=1)
        store(b, jnp.concatenate((top, low), axis=0))


def unpack(gathered, store):
    lanes = gathered.shape[2] // 2
    for b in range(gathered.shape[0] // 2):
        one, two = gathered[2 * b], gathered[2 * b + 1]
        top = jnp.concatenate((one[:, :lanes], two[:, :lanes]), axis=1)
        low = jnp.concatenate((one[:, lanes:], two[:, lanes:]), axis=1)
        store(b, jnp.concatenate((top, low), axis=0))


def dot_lanes(a, b):
    return lax.dot_general(a, b, (((1,), (1,)), ((), ())), preferred_element_type=jnp.float32)


def start_kernel(right_ref, message_ref):
    message_ref[...] = pack(right_ref[0], message_ref.shape[0])


def solve_kernel(gathered_ref, inverse_ref, result_ref, message_ref, flat_ref):
    def store(b, block):
        flat_ref[:, b * BS : (b + 1) * BS] = block

    unpack(gathered_ref, store)
    result = dot_lanes(flat_ref[...], inverse_ref[...])
    result_ref[...] = result
    message_ref[...] = pack(result, message_ref.shape[0])


def below_part(near_ref, far_ref, k, tier, tiers):
    ref = near_ref if k < 2 else far_ref
    return ref.at[k % 2 * tiers + tier]


def select_kernel(position_ref, near_ref, far_ref, out_ref):
    positions = position_ref[...]
    part = near_ref.shape[2] // BS
    tiers = near_ref.shape[0] // 2
    for j in range(out_ref.shape[2] // BS):
        at = positions[0, j]
        for k in range(RB // part):

            @pl.when(at // part == k)
            def _():
                columns = pl.ds(pl.multiple_of(at % part * BS, BS), BS)
                block = below_part(near_ref, far_ref, k, tiers - 1, tiers)[:, columns]
                out_ref[0, :, j * BS : (j + 1) * BS] = block


def join(mine, other, core):
    first = jnp.where(core == 0, mine, other)
    second = jnp.where(core == 0, other, mine)
    return jnp.concatenate((first, second), axis=1)


def position():
    own = lax.axis_index("sn")
    return own % 2, own // 2 % 4, own // 8 % 2


def product_kernel(corner, coupled_ref, *refs):
    third, out_ref = refs[:4], refs[-1]
    core, y, z = position()
    total = refs[4][0] if corner else None
    for g, ref in enumerate(third):
        picked = []
        for e in (3,) if corner else range(ref.shape[0]):
            block = (z ^ (e // 2)) * 4 + (y ^ (e % 2 * 2 + g % 2))
            columns = coupled_ref[0, :, pl.ds(pl.multiple_of(block * BS, BS), BS)]
            half = columns.shape[1] // 2
            first = core == g // 2
            picked.append(jnp.where(first, columns[:, :half], columns[:, half:]))
        rows = ref[...].reshape(ref.shape[0] * ref.shape[1], ref.shape[2])
        picked = picked[0] if corner else jnp.concatenate(picked, axis=1)
        term = jnp.dot(picked, rows, preferred_element_type=jnp.float32)
        total = term if total is None else total + term
    out_ref[0] = total.astype(out_ref.dtype)


def final_kernel(
    pieces, gathered_ref, third_ref, fourth_ref, first_result_ref, second_result_ref, *refs
):
    parent, parent_other = refs[:pieces], refs[pieces : 2 * pieces]
    out_ref, flat_ref, coupled_ref, last_ref = refs[2 * pieces :]
    core, y, z = position()
    half = gathered_ref.shape[1] // 2
    devices = gathered_ref.shape[0]

    def store(b, block):
        flat_ref[:, b * BS : (b + 1) * BS] = block

    def store_last(b, block):
        last_ref[:, b * BS : (b + 1) * BS] = block

    unpack(gathered_ref[:, :half], store)
    in_plane = pl.ds(pl.multiple_of(z * (devices // 2), devices // 2), devices // 2)
    unpack(gathered_ref[in_plane, half:], store_last)
    out_ref[0] = first_result_ref[...]
    out_ref[1] = second_result_ref[...]
    out_ref[2] = dot_lanes(flat_ref[...], third_ref[...])
    for e in range(pieces):
        mine = dot_lanes(flat_ref[...], parent[e][0])
        other = dot_lanes(flat_ref[...], parent_other[e][0])
        columns = pl.ds(pl.multiple_of((y ^ e) * BS, BS), BS)
        coupled_ref[:, columns] = join(mine, other, core)
    update = last_ref[...].astype(jnp.float32) - coupled_ref[...]
    out_ref[3] = dot_lanes(update.astype(jnp.bfloat16), fourth_ref[...])


def place(chosen, own_block):
    found, base = chosen, NB
    for l in range(1, LEVELS - 1):
        count = NB >> l
        mine = own_block // count * count
        at = chosen - l * NB - mine + base
        if l == LEVELS - 2:
            at = jnp.full_like(chosen, base)
        found = jnp.where(chosen // NB == l, at, found)
        base += count
    return found


def update_kernel(tiers, kept, parts, index_ref, gathered_ref, right_ref, *refs):
    if kept:
        other_ref, refs = refs[0], refs[1:]
    below = refs[:parts] if kept else refs[:2]
    refs = refs[len(below) :]
    known_ref, flat_ref = refs[-2], refs[-1]
    base = 0
    if not kept:
        base = refs[0].shape[0]
        known_ref[:base] = refs[0][...]
        refs = refs[1:]
    message_ref = refs[0]

    def store(b, block):
        known_ref[base + b] = block

    if kept:
        unpack_cores(gathered_ref, other_ref, store)
    else:
        unpack(gathered_ref, store)
    if kept:
        refs[1][...] = known_ref[...]
    else:
        known_ref[known_ref.shape[0] - 1] = jnp.zeros(known_ref.shape[1:], known_ref.dtype)
    places = index_ref[...]
    quarter = RB // parts
    slot = 0
    packed = []
    for t, tier in enumerate(tiers):
        total = right_ref[tier]
        for k in range(parts):
            ref = below[k] if kept else below_part(*below, k, t, len(tiers))
            for p in range(quarter):
                block = known_ref[places[tier - 1, k * quarter + p]]
                flat_ref[slot, :, p * BS : (p + 1) * BS] = block
            total = total - dot_lanes(flat_ref[slot], ref[...])
            slot += 1
        packed.append(pack(total, message_ref.shape[0]))
    message_ref[...] = jnp.concatenate(packed, axis=1)


VMEM = pl.BlockSpec(memory_space=pltpu.VMEM)


def held(*arrays):
    return [pltpu.with_memory_space_constraint(array, pltpu.HBM) for array in arrays]


def call(kernel, name, outs, scratch, *args, flops=20_000_000):
    return pl.pallas_call(
        kernel,
        out_shape=outs,
        in_specs=[VMEM] * len(args),
        out_specs=[VMEM] * len(outs),
        scratch_shapes=scratch,
        cost_estimate=pl.CostEstimate(flops=flops, bytes_accessed=flops // 20, transcendentals=0),
        compiler_params=pltpu.CompilerParams(vmem_limit_bytes=16 * 2**20),
        name=name,
    )(*args)


def on_device(
    right_sides,
    factor_below,
    row_blocks,
    inverse_top,
    inverse_second,
    inverse_third,
    inverse_fourth,
):
    _, rows, columns = right_sides.shape
    right_sides = jnp.swapaxes(right_sides, 1, 2)
    devices = lax.axis_size("sn")
    groups = lax.axis_size("rhs")
    column_group = lax.axis_index("rhs")
    own = lax.axis_index("sn")
    f32, bf16 = jnp.float32, jnp.bfloat16
    shape = jax.ShapeDtypeStruct
    message = (columns // 2, 2 * rows)
    members = [devices >> l for l in range(LEVELS)]
    barrier = lax.optimization_barrier

    def gather(copies):
        n = copies.shape[0]
        sets = None
        if n < devices:
            sets = [list(range(s, s + n)) for s in range(0, devices, n)]
        return lax.all_to_all(copies, "sn", 0, 0, axis_index_groups=sets)

    def gather_core(copies):
        sets = [[2 * k + c for k in range(devices // 2)] for c in range(2)]
        return lax.all_to_all(copies, "sn", 0, 0, axis_index_groups=sets)

    def swap_group(part, bit):
        return lax.ppermute(part, "rhs", [(i, i ^ bit) for i in range(groups)])

    def swap(part, bit):
        return lax.ppermute(part, "sn", [(i, i ^ bit) for i in range(devices)])

    core, y_low, y_high, z_low = 1, 2, 4, 8

    def over_y(part):
        return [part] + [swap(part, bits) for bits in (y_low, y_high, y_low + y_high)]

    own_block = own * rows // BS
    chosen = lax.dynamic_index_in_dim(row_blocks, own_block, 1, keepdims=False)
    places = place(chosen, own_block)
    quarter = RB // groups
    part = jnp.arange(groups)
    source = (column_group ^ part)[:, None] == part[None, :]
    listed = places.reshape(LEVELS - 1, 1, groups, quarter)
    places = jnp.sum(jnp.where(source[None, :, :, None], listed, 0), axis=2)
    places = places.reshape(LEVELS - 1, RB)
    count = NB >> (LEVELS - 2)
    parent = (LEVELS - 2) * NB + own_block // count * count + jnp.arange(count)
    listed = jnp.arange(RB)
    turned = (column_group ^ listed // quarter) * quarter + listed % quarter
    hit = chosen[LEVELS - 2][None, :] == parent[:, None]
    positions = jnp.sum(jnp.where(hit, turned[None, :], 0), axis=1)[None].astype(jnp.int32)
    places, positions, right_sides = barrier((places, positions, right_sides))

    first_below, rest_below = factor_below[0], factor_below[1:]
    first_got = [swap_group(first_below, bits) for bits in (1, 3)]
    rest_got = swap_group(rest_below, 1)
    third = inverse_third[None]
    far, near = swap(third, y_high), swap(third, z_low)

    (copies,) = call(start_kernel, "start", [shape((members[0], *message), bf16)], [], right_sides)
    gathered = gather(copies)
    first_result, copies = call(
        solve_kernel,
        "solve0",
        [shape((columns, rows), f32), shape((devices // 2, *message), bf16)],
        [pltpu.VMEM((columns, members[0] * rows), bf16)],
        gathered,
        inverse_top,
    )

    copies, far, near, first_got, rest_got = barrier((copies, far, near, first_got, rest_got))
    first_parts = (first_below, first_got[0], swap_group(first_below, 2), first_got[1])
    rest_below = jnp.concatenate((rest_below, rest_got))
    rest_far = swap_group(rest_below, 2)
    third = jnp.concatenate((third, far, near))
    third_got = swap(third, y_low)
    corner = swap(far, z_low)

    gathered = gather_core(copies)
    gathered, corner, first_parts = barrier((gathered, corner, first_parts))
    other = swap(gathered, core)
    copies, known = call(
        functools.partial(update_kernel, (1,), True, groups),
        "update1",
        [shape((members[1], *message), bf16), shape((NB, columns, BS), bf16)],
        [pltpu.VMEM((NB, columns, BS), bf16), pltpu.VMEM((groups, columns, RB // groups * BS), bf16)],
        places,
        gathered,
        right_sides,
        other,
        *first_parts,
        flops=20_000,
    )

    copies, third_got, corner = barrier((copies, third_got, corner))
    corner = [corner, swap(corner, y_low)]
    third = [third, third_got]
    third = third + [swap(part, core) for part in third]
    corner = corner + [swap(part, core) for part in corner]
    (coupled,) = call(
        select_kernel, "select", [shape((1, rows, count * BS), bf16)], [], positions, rest_below, rest_far
    )

    (partial,) = call(
        functools.partial(product_kernel, False),
        "product",
        [shape(coupled.shape, f32)],
        [],
        coupled,
        *held(*third),
    )
    gathered = gather(copies)
    gathered, coupled, partial = barrier((gathered, coupled, partial))
    second_result, copies = call(
        solve_kernel,
        "solve1",
        [shape((columns, rows), f32), shape((members[1], *message), bf16)],
        [pltpu.VMEM((columns, members[1] * rows), bf16)],
        gathered,
        inverse_second,
    )

    (coupled,) = call(
        functools.partial(product_kernel, True),
        "corner",
        [shape(coupled.shape, bf16)],
        [],
        coupled,
        *corner,
        partial,
    )
    coupled = over_y(coupled)

    gathered = gather(copies)
    blocks = NB + NB // 2 + 1
    (copies,) = call(
        functools.partial(update_kernel, (2, 3), False, groups),
        "update2",
        [shape((members[2], 2 * message[0], message[1]), bf16)],
        [pltpu.VMEM((blocks, columns, BS), bf16), pltpu.VMEM((2 * groups, columns, RB // groups * BS), bf16)],
        places,
        gathered,
        right_sides,
        rest_below,
        rest_far,
        known,
    )

    coupled_other = [swap(part, core) for part in coupled]

    gathered = gather(copies)
    (out,) = call(
        functools.partial(final_kernel, len(coupled)),
        "final",
        [shape((LEVELS, columns, rows), f32)],
        [
            pltpu.VMEM((columns, members[2] * rows), bf16),
            pltpu.VMEM((columns, members[3] * rows), f32),
            pltpu.VMEM((columns, members[3] * rows), bf16),
        ],
        gathered,
        inverse_third,
        inverse_fourth,
        first_result,
        second_result,
        *coupled,
        *coupled_other,
    )
    return jnp.swapaxes(out, 1, 2)


def solution(mesh):
    in_specs = (
        P(None, "sn", "rhs"),
        P(None, "sn", "rhs"),
        P(),
        P("sn", None),
        P("sn", None),
        P("sn", None),
        P("sn", None),
    )
    out_specs = P(None, "sn", "rhs")
    return jax.shard_map(
        on_device, mesh=mesh, in_specs=in_specs, out_specs=out_specs, check_vma=False
    )
```

```python
import functools

import jax
import jax.numpy as jnp
from jax import lax
from jax.experimental import pallas as pl
from jax.experimental.pallas import tpu as pltpu
from jax.sharding import PartitionSpec as P

BS = 128
NB = 32
LEVELS = 4
RB = 32


def pack(block, copies):
    half = block.shape[0] // 2
    packed = jnp.concatenate((block[:half], block[half:]), axis=1).astype(jnp.bfloat16)
    return jnp.broadcast_to(packed[None], (copies, *packed.shape))


def unpack_cores(mine_ref, other_ref, store):
    core = lax.axis_index("sn") % 2
    lanes = mine_ref.shape[2] // 2
    for b in range(mine_ref.shape[0]):
        one = jnp.where(core == 0, mine_ref[b], other_ref[b])
        two = jnp.where(core == 0, other_ref[b], mine_ref[b])
        top = jnp.concatenate((one[:, :lanes], two[:, :lanes]), axis=1)
        low = jnp.concatenate((one[:, lanes:], two[:, lanes:]), axis=1)
        store(b, jnp.concatenate((top, low), axis=0))


def unpack(gathered, store):
    lanes = gathered.shape[2] // 2
    for b in range(gathered.shape[0] // 2):
        one, two = gathered[2 * b], gathered[2 * b + 1]
        top = jnp.concatenate((one[:, :lanes], two[:, :lanes]), axis=1)
        low = jnp.concatenate((one[:, lanes:], two[:, lanes:]), axis=1)
        store(b, jnp.concatenate((top, low), axis=0))


def dot_lanes(a, b):
    return lax.dot_general(a, b, (((1,), (1,)), ((), ())), preferred_element_type=jnp.float32)


def start_kernel(right_ref, message_ref):
    message_ref[...] = pack(right_ref[0], message_ref.shape[0])


def solve_kernel(gathered_ref, inverse_ref, result_ref, message_ref, flat_ref):
    def store(b, block):
        flat_ref[:, b * BS : (b + 1) * BS] = block

    unpack(gathered_ref, store)
    result = dot_lanes(flat_ref[...], inverse_ref[...])
    result_ref[...] = result
    message_ref[...] = pack(result, message_ref.shape[0])


def below_part(near_ref, far_ref, k, tier, tiers):
    ref = near_ref if k < 2 else far_ref
    return ref.at[k % 2 * tiers + tier]


def select_kernel(position_ref, near_ref, far_ref, out_ref):
    positions = position_ref[...]
    part = near_ref.shape[2] // BS
    tiers = near_ref.shape[0] // 2
    for j in range(out_ref.shape[2] // BS):
        at = positions[0, j]
        for k in range(RB // part):

            @pl.when(at // part == k)
            def _():
                columns = pl.ds(pl.multiple_of(at % part * BS, BS), BS)
                block = below_part(near_ref, far_ref, k, tiers - 1, tiers)[:, columns]
                out_ref[0, :, j * BS : (j + 1) * BS] = block


def join(mine, other, core):
    first = jnp.where(core == 0, mine, other)
    second = jnp.where(core == 0, other, mine)
    return jnp.concatenate((first, second), axis=1)


def position():
    own = lax.axis_index("sn")
    return own % 2, own // 2 % 4, own // 8 % 2


def product_kernel(corner, coupled_ref, *refs):
    third, out_ref = refs[:4], refs[-1]
    core, y, z = position()
    total = refs[4][0] if corner else None
    for g, ref in enumerate(third):
        picked = []
        for e in (3,) if corner else range(ref.shape[0]):
            block = (z ^ (e // 2)) * 4 + (y ^ (e % 2 * 2 + g % 2))
            columns = coupled_ref[0, :, pl.ds(pl.multiple_of(block * BS, BS), BS)]
            half = columns.shape[1] // 2
            first = core == g // 2
            picked.append(jnp.where(first, columns[:, :half], columns[:, half:]))
        rows = ref[...].reshape(ref.shape[0] * ref.shape[1], ref.shape[2])
        picked = picked[0] if corner else jnp.concatenate(picked, axis=1)
        term = jnp.dot(picked, rows, preferred_element_type=jnp.float32)
        total = term if total is None else total + term
    out_ref[0] = total.astype(out_ref.dtype)


def final_kernel(
    pieces, gathered_ref, third_ref, fourth_ref, first_result_ref, second_result_ref, *refs
):
    parent, parent_other = refs[:pieces], refs[pieces : 2 * pieces]
    out_ref, flat_ref, coupled_ref, last_ref = refs[2 * pieces :]
    core, y, z = position()
    half = gathered_ref.shape[1] // 2
    devices = gathered_ref.shape[0]

    def store(b, block):
        flat_ref[:, b * BS : (b + 1) * BS] = block

    def store_last(b, block):
        last_ref[:, b * BS : (b + 1) * BS] = block

    unpack(gathered_ref[:, :half], store)
    in_plane = pl.ds(pl.multiple_of(z * (devices // 2), devices // 2), devices // 2)
    unpack(gathered_ref[in_plane, half:], store_last)
    out_ref[0] = first_result_ref[...]
    out_ref[1] = second_result_ref[...]
    out_ref[2] = dot_lanes(flat_ref[...], third_ref[...])
    for e in range(pieces):
        mine = dot_lanes(flat_ref[...], parent[e][0])
        other = dot_lanes(flat_ref[...], parent_other[e][0])
        columns = pl.ds(pl.multiple_of((y ^ e) * BS, BS), BS)
        coupled_ref[:, columns] = join(mine, other, core)
    update = last_ref[...].astype(jnp.float32) - coupled_ref[...]
    out_ref[3] = dot_lanes(update.astype(jnp.bfloat16), fourth_ref[...])


def place(chosen, own_block):
    found, base = chosen, NB
    for l in range(1, LEVELS - 1):
        count = NB >> l
        mine = own_block // count * count
        at = chosen - l * NB - mine + base
        if l == LEVELS - 2:
            at = jnp.full_like(chosen, base)
        found = jnp.where(chosen // NB == l, at, found)
        base += count
    return found


def update_kernel(tiers, kept, parts, index_ref, gathered_ref, right_ref, *refs):
    if kept:
        other_ref, refs = refs[0], refs[1:]
    below = refs[:parts] if kept else refs[:2]
    refs = refs[len(below) :]
    known_ref, flat_ref = refs[-2], refs[-1]
    base = 0
    if not kept:
        base = refs[0].shape[0]
        known_ref[:base] = refs[0][...]
        refs = refs[1:]
    message_ref = refs[0]

    def store(b, block):
        known_ref[base + b] = block

    if kept:
        unpack_cores(gathered_ref, other_ref, store)
    else:
        unpack(gathered_ref, store)
    if kept:
        refs[1][...] = known_ref[...]
    else:
        known_ref[known_ref.shape[0] - 1] = jnp.zeros(known_ref.shape[1:], known_ref.dtype)
    places = index_ref[...]
    quarter = RB // parts
    slot = 0
    packed = []
    for t, tier in enumerate(tiers):
        total = right_ref[tier]
        for k in range(parts):
            ref = below[k] if kept else below_part(*below, k, t, len(tiers))
            for p in range(quarter):
                block = known_ref[places[tier - 1, k * quarter + p]]
                flat_ref[slot, :, p * BS : (p + 1) * BS] = block
            total = total - dot_lanes(flat_ref[slot], ref[...])
            slot += 1
        packed.append(pack(total, message_ref.shape[0]))
    message_ref[...] = jnp.concatenate(packed, axis=1)


VMEM = pl.BlockSpec(memory_space=pltpu.VMEM)


def held(*arrays):
    return [pltpu.with_memory_space_constraint(array, pltpu.HBM) for array in arrays]


def call(kernel, name, outs, scratch, *args, flops=20_000_000):
    return pl.pallas_call(
        kernel,
        out_shape=outs,
        in_specs=[VMEM] * len(args),
        out_specs=[VMEM] * len(outs),
        scratch_shapes=scratch,
        cost_estimate=pl.CostEstimate(flops=flops, bytes_accessed=flops // 20, transcendentals=0),
        compiler_params=pltpu.CompilerParams(vmem_limit_bytes=16 * 2**20),
        name=name,
    )(*args)


def on_device(
    right_sides,
    factor_below,
    row_blocks,
    inverse_top,
    inverse_second,
    inverse_third,
    inverse_fourth,
):
    _, rows, columns = right_sides.shape
    right_sides = jnp.swapaxes(right_sides, 1, 2)
    devices = lax.axis_size("sn")
    groups = lax.axis_size("rhs")
    column_group = lax.axis_index("rhs")
    own = lax.axis_index("sn")
    f32, bf16 = jnp.float32, jnp.bfloat16
    shape = jax.ShapeDtypeStruct
    message = (columns // 2, 2 * rows)
    members = [devices >> l for l in range(LEVELS)]
    barrier = lax.optimization_barrier

    def gather(copies):
        n = copies.shape[0]
        sets = None
        if n < devices:
            sets = [list(range(s, s + n)) for s in range(0, devices, n)]
        return lax.all_to_all(copies, "sn", 0, 0, axis_index_groups=sets)

    def gather_core(copies):
        sets = [[2 * k + c for k in range(devices // 2)] for c in range(2)]
        return lax.all_to_all(copies, "sn", 0, 0, axis_index_groups=sets)

    def swap_group(part, bit):
        return lax.ppermute(part, "rhs", [(i, i ^ bit) for i in range(groups)])

    def swap(part, bit):
        return lax.ppermute(part, "sn", [(i, i ^ bit) for i in range(devices)])

    core, y_low, y_high, z_low = 1, 2, 4, 8

    def over_y(part):
        return [part] + [swap(part, bits) for bits in (y_low, y_high, y_low + y_high)]

    own_block = own * rows // BS
    chosen = lax.dynamic_index_in_dim(row_blocks, own_block, 1, keepdims=False)
    places = place(chosen, own_block)
    quarter = RB // groups
    part = jnp.arange(groups)
    source = (column_group ^ part)[:, None] == part[None, :]
    listed = places.reshape(LEVELS - 1, 1, groups, quarter)
    places = jnp.sum(jnp.where(source[None, :, :, None], listed, 0), axis=2)
    places = places.reshape(LEVELS - 1, RB)
    count = NB >> (LEVELS - 2)
    parent = (LEVELS - 2) * NB + own_block // count * count + jnp.arange(count)
    listed = jnp.arange(RB)
    turned = (column_group ^ listed // quarter) * quarter + listed % quarter
    hit = chosen[LEVELS - 2][None, :] == parent[:, None]
    positions = jnp.sum(jnp.where(hit, turned[None, :], 0), axis=1)[None].astype(jnp.int32)
    places, positions, right_sides = barrier((places, positions, right_sides))

    first_below, rest_below = factor_below[0], factor_below[1:]
    first_got = [swap_group(first_below, bits) for bits in (1, 3)]
    rest_got = swap_group(rest_below, 1)
    third = inverse_third[None]
    far, near = swap(third, y_high), swap(third, z_low)

    (copies,) = call(start_kernel, "start", [shape((members[0], *message), bf16)], [], right_sides)
    gathered = gather(copies)
    first_result, copies = call(
        solve_kernel,
        "solve0",
        [shape((columns, rows), f32), shape((devices // 2, *message), bf16)],
        [pltpu.VMEM((columns, members[0] * rows), bf16)],
        gathered,
        inverse_top,
    )

    copies, far, near, first_got, rest_got = barrier((copies, far, near, first_got, rest_got))
    first_parts = (first_below, first_got[0], swap_group(first_below, 2), first_got[1])
    rest_below = jnp.concatenate((rest_below, rest_got))
    rest_far = swap_group(rest_below, 2)
    third = jnp.concatenate((third, far, near))
    third_got = swap(third, y_low)
    corner = swap(far, z_low)

    gathered = gather_core(copies)
    gathered, corner, first_parts = barrier((gathered, corner, first_parts))
    other = swap(gathered, core)
    copies, known = call(
        functools.partial(update_kernel, (1,), True, groups),
        "update1",
        [shape((members[1], *message), bf16), shape((NB, columns, BS), bf16)],
        [pltpu.VMEM((NB, columns, BS), bf16), pltpu.VMEM((groups, columns, RB // groups * BS), bf16)],
        places,
        gathered,
        right_sides,
        other,
        *first_parts,
        flops=20_000,
    )

    copies, third_got, corner = barrier((copies, third_got, corner))
    corner = [corner, swap(corner, y_low)]
    third = [third, third_got]
    third = third + [swap(part, core) for part in third]
    corner = corner + [swap(part, core) for part in corner]
    (coupled,) = call(
        select_kernel, "select", [shape((1, rows, count * BS), bf16)], [], positions, rest_below, rest_far
    )

    (partial,) = call(
        functools.partial(product_kernel, False),
        "product",
        [shape(coupled.shape, f32)],
        [],
        coupled,
        *held(*third),
    )
    gathered = gather(copies)
    gathered, coupled, partial, corner = barrier((gathered, coupled, partial, corner))
    second_result, copies = call(
        solve_kernel,
        "solve1",
        [shape((columns, rows), f32), shape((members[1], *message), bf16)],
        [pltpu.VMEM((columns, members[1] * rows), bf16)],
        gathered,
        inverse_second,
    )

    (coupled,) = call(
        functools.partial(product_kernel, True),
        "corner",
        [shape(coupled.shape, bf16)],
        [],
        coupled,
        *corner,
        partial,
    )
    coupled = over_y(coupled)

    gathered = gather(copies)
    blocks = NB + NB // 2 + 1
    (copies,) = call(
        functools.partial(update_kernel, (2, 3), False, groups),
        "update2",
        [shape((members[2], 2 * message[0], message[1]), bf16)],
        [pltpu.VMEM((blocks, columns, BS), bf16), pltpu.VMEM((2 * groups, columns, RB // groups * BS), bf16)],
        places,
        gathered,
        right_sides,
        rest_below,
        rest_far,
        known,
    )

    coupled_other = [swap(part, core) for part in coupled]

    gathered = gather(copies)
    (out,) = call(
        functools.partial(final_kernel, len(coupled)),
        "final",
        [shape((LEVELS, columns, rows), f32)],
        [
            pltpu.VMEM((columns, members[2] * rows), bf16),
            pltpu.VMEM((columns, members[3] * rows), f32),
            pltpu.VMEM((columns, members[3] * rows), bf16),
        ],
        gathered,
        inverse_third,
        inverse_fourth,
        first_result,
        second_result,
        *coupled,
        *coupled_other,
    )
    return jnp.swapaxes(out, 1, 2)


def solution(mesh):
    in_specs = (
        P(None, "sn", "rhs"),
        P(None, "sn", "rhs"),
        P(),
        P("sn", None),
        P("sn", None),
        P("sn", None),
        P("sn", None),
    )
    out_specs = P(None, "sn", "rhs")
    return jax.shard_map(
        on_device, mesh=mesh, in_specs=in_specs, out_specs=out_specs, check_vma=False
    )
```
